1024 devices in a mesh: row: 64 (over x, z_lo, core), col: 16 (over y, z_hi).
Axes of the slice: x: 4, y: 4, z: 32 (z_hi: 4, z_lo: 8; z = z_hi * 8 + z_lo), core: 2. Of those that a mesh axis runs over, the one named last changes fastest.
Arguments:
- features: bfloat16 [262144, 128], P(('col', 'row')), may hold values from -6 to 6
- adj_blocks: bfloat16 [64, 16, 64, 128, 128], P('row', 'col'), may hold values from -0.09375 to 0.09375
- block_coords: int32 [64, 16, 2, 64], P('row', 'col'), may hold values from 0 to 127, as said below
- counts: int32 [64, 16], replicated, may hold values from 4 to 64, as said below
- weight: bfloat16 [128, 256], replicated, may hold values from -0.5 to 0.5
- cotangent: bfloat16 [262144, 256], P(('row', 'col')), may hold values from -0.01171875 to 0.01171875
Outputs:
- activated: bfloat16 [262144, 256], P(('row', 'col'))
- weight_grad: float32 [128, 256], replicated
The draws below stay inside these ranges and needn't reach their ends.
Inputs may be any that keep to these rules, and one draw needn't show every extreme that they name: `block_coords`: slots at or past a tile's count hold values that take no part. `block_coords`: block rows are below 32, block columns below 128. `counts`: each count is 64 divided by a power of two.
All inputs are finite; a program needn't handle non-finite values.
Results may differ from the reference program's by a relative error of at most 0.0052.
Values may be sent and summed in bfloat16 or wider, within the bound.
A program may use at most 32 MiB of HBM per device.

```python
import jax
import jax.numpy as jnp
from jax import lax

F = 128
HID = 256
BLOCK = 128
ROWS_DEV = 256
MAXB = 64
GROUP = 32
NODES = 262144
RBLK = 32
CBLK = 128
N_ROW = 64
N_COL = 16


def draw_block_coords(key, part):
    key = jax.random.fold_in(key, 11)
    row_key, col_key = jax.random.split(key)
    block_rows = jax.random.randint(row_key, (N_ROW, N_COL, 1, MAXB), 0, RBLK)
    block_cols = jax.random.randint(col_key, (N_ROW, N_COL, 1, MAXB), 0, CBLK)
    return jnp.concatenate([block_rows, block_cols], axis=2).astype(jnp.int32)


def draw_counts(key, part):
    key = jax.random.fold_in(key, 23)
    level_key, first_key, second_key = jax.random.split(key, 3)
    tile_total = N_ROW * N_COL
    levels = jax.random.randint(level_key, (tile_total,), 0, 5)
    loads = MAXB // jnp.power(2, levels)
    busiest = jax.random.randint(first_key, (), 0, tile_total)
    lightest = (busiest + 1 + jax.random.randint(second_key, (), 0, tile_total - 1)) % tile_total
    position = jnp.arange(tile_total)
    loads = jnp.where(position == busiest, MAXB, loads)
    loads = jnp.where(position == lightest, MAXB // 16, loads)
    return loads.reshape(N_ROW, N_COL).astype(jnp.int32)


def steps_of(own_key, dims, cuts, smallest, largest):
    factor_of = 1.0
    for dim, shards_of in cuts:
        draws = jax.random.uniform(jax.random.fold_in(jax.random.fold_in(own_key, 6), dim), (shards_of,), jnp.float32, smallest / len(cuts), largest / len(cuts))
        factor_of = factor_of * jnp.repeat(jnp.exp(draws), dims[dim] // shards_of).reshape((-1,) + (1,) * (len(dims) - 1 - dim))
    return factor_of


def bell_draw(stream_key, extent, width, limit, cuts=(), kind=jnp.bfloat16):
    array = width * jax.random.normal(stream_key, extent, jnp.float32)
    if cuts:
        array = array * steps_of(stream_key, extent, cuts, -0.22, 0.18)
    return jnp.clip(array, -limit, limit).astype(kind)


def setup_inputs(seed: int = 0) -> dict:
    key_list = jax.random.split(jax.random.key(seed), 7)
    return {
        "features": bell_draw(key_list[0], (NODES, F), 1.0, 6.0, ((0, 1024),)),
        "adj_blocks": bell_draw(key_list[1], (N_ROW, N_COL, MAXB, BLOCK, BLOCK), (BLOCK * BLOCK * MAXB // ROWS_DEV) ** -0.5, 0.09375, ((0, 64), (1, 16))),
        "block_coords": draw_block_coords(jax.random.fold_in(key_list[6], 71), 0),
        "counts": draw_counts(jax.random.fold_in(key_list[6], 71), 0),
        "weight": bell_draw(key_list[4], (F, HID), F ** -0.5, 0.5),
        "cotangent": bell_draw(key_list[5], (NODES, HID), NODES ** -0.5, 0.01171875, ((0, 1024),)),
    }


def silu_slope(preact, sigmoid_value):
    return sigmoid_value * (1.0 + preact * (1.0 - sigmoid_value))


def reference(features, adj_blocks, block_coords, counts, weight, cotangent):
    grid_rows, grid_cols, slot_count, block_size, _ = adj_blocks.shape
    feature_width = features.shape[1]
    feature_blocks = features.reshape(-1, block_size, feature_width)
    row_tile_blocks = features.shape[0] // grid_rows // block_size
    col_tile_blocks = features.shape[0] // grid_cols // block_size

    def one_tile(running, tile_index):
        row_index = tile_index // grid_cols
        col_index = tile_index % grid_cols
        tile_blocks = adj_blocks[row_index, col_index]
        tile_coords = block_coords[row_index, col_index]
        live_count = counts[row_index, col_index]

        def advance(turn_index, partial_value):
            start_slot = turn_index * GROUP
            alive_mask = start_slot + jnp.arange(GROUP, dtype=jnp.int32) < live_count
            chosen = lax.dynamic_slice_in_dim(tile_blocks, start_slot, GROUP, 0).astype(jnp.float32)
            target_rows = lax.dynamic_slice_in_dim(tile_coords[0], start_slot, GROUP, 0) + row_index * row_tile_blocks
            source_cols = lax.dynamic_slice_in_dim(tile_coords[1], start_slot, GROUP, 0) + col_index * col_tile_blocks
            inputs = jnp.take(feature_blocks, source_cols.astype(jnp.int32), axis=0).astype(jnp.float32)
            products = jnp.einsum("gab,gbf->gaf", chosen, inputs)
            products = jnp.where(alive_mask[:, None, None], products, 0.0)
            return partial_value.at[target_rows.astype(jnp.int32)].add(products)

        turns = (live_count + GROUP - 1) // GROUP
        return lax.fori_loop(0, turns, advance, running), None

    running = jnp.zeros((features.shape[0] // block_size, block_size, feature_width), jnp.float32)
    running, _ = lax.scan(one_tile, running, jnp.arange(grid_rows * grid_cols, dtype=jnp.int32))
    aggregate = running.reshape(features.shape[0], feature_width)
    rounded = aggregate.astype(jnp.bfloat16)
    preact = jnp.dot(rounded, weight, preferred_element_type=jnp.float32)
    sigmoid_value = jax.nn.sigmoid(preact)
    activated = (preact * sigmoid_value).astype(jnp.bfloat16)
    slope_grad = (cotangent.astype(jnp.float32) * silu_slope(preact, sigmoid_value)).astype(jnp.bfloat16)
    weight_grad = jnp.dot(rounded.T, slope_grad, preferred_element_type=jnp.float32)
    return activated, weight_grad
```

```python
import jax
import jax.numpy as jnp
from jax import lax
from jax.experimental import pallas as pl
from jax.experimental.pallas import tpu as pltpu
from jax.sharding import PartitionSpec as P

NX, NZ, NC = 4, 8, 2
NY, NH = 4, 4
BLOCK = 128
GROUP = 4
MESH = pl.DeviceIdType.MESH


def remote(src, dst, send_sem, recv_sem, device):
    return pltpu.make_async_remote_copy(
        src_ref=src, dst_ref=dst, send_sem=send_sem, recv_sem=recv_sem, device_id=device, device_id_type=MESH
    )


def gather_kernel(
    f_ref, out_ref, own_sem, zu_s, zu_r, zd_s, zd_r, xs_s, xs_r, xf_s, xf_r, cc_s, cc_r
):
    half = f_ref.shape[0] // 2
    r = lax.axis_index("row")
    x, z, core = r // (NZ * NC), (r // NC) % NZ, r % NC

    def slot(xx, zz, cc=None):
        return ((xx % NX) * NZ + zz) * NC + (core if cc is None else cc)

    up, down = {"row": slot(x, z + 1)}, {"row": slot(x, z - 1)}
    right, left = {"row": slot(x + 1, z)}, {"row": slot(x - 1, z)}
    other = {"row": slot(x, z, 1 - core)}

    def z_up(d, src=None):
        s = slot(x, z - d)
        return remote(out_ref.at[s] if src is None else src, out_ref.at[s], zu_s.at[d], zu_r.at[d], up)

    def z_down(d, src=None):
        s = slot(x, z + d)
        return remote(out_ref.at[s] if src is None else src, out_ref.at[s], zd_s.at[d], zd_r.at[d], down)

    def x_copy(zz, way, src=None):
        s = slot(x, zz)
        return remote(
            out_ref.at[s] if src is None else src,
            out_ref.at[s],
            xs_s.at[way, zz],
            xs_r.at[way, zz],
            right if way == 0 else left,
        )

    def x_forward(zz, way):
        s = slot(x - 1 if way == 0 else x + 1, zz)
        rows = pl.ds(way * half, half)
        return remote(
            out_ref.at[s, rows],
            out_ref.at[s, rows],
            xf_s.at[way, zz],
            xf_r.at[way, zz],
            right if way == 0 else left,
        )

    def x_arrival(zz, way):
        s = slot(x - 1 if way == 0 else x + 1, zz)
        return remote(out_ref.at[s], out_ref.at[s], xs_s.at[way, zz], xs_r.at[way, zz], right)

    def f_arrival(zz, way):
        s = slot(x + 2, zz)
        rows = pl.ds(way * half, half)
        return remote(out_ref.at[s, rows], out_ref.at[s, rows], xf_s.at[way, zz], xf_r.at[way, zz], right)

    def cross(dx, zz, src=None):
        s = slot(x + dx, zz)
        return remote(out_ref.at[s] if src is None else src, out_ref.at[s], cc_s.at[dx, zz], cc_r.at[dx, zz], other)

    def cross_arrival(dx, zz):
        s = slot(x + dx, zz, 1 - core)
        return remote(out_ref.at[s], out_ref.at[s], cc_s.at[dx, zz], cc_r.at[dx, zz], other)

    has_up, has_down = z < NZ - 1, z > 0
    barrier = pltpu.get_barrier_semaphore()
    for device in (right, left, other):
        pl.semaphore_signal(barrier, inc=1, device_id=device, device_id_type=MESH)

    @pl.when(has_up)
    def _():
        pl.semaphore_signal(barrier, inc=1, device_id=up, device_id_type=MESH)

    @pl.when(has_down)
    def _():
        pl.semaphore_signal(barrier, inc=1, device_id=down, device_id_type=MESH)

    own = pltpu.make_async_copy(f_ref, out_ref.at[r], own_sem)
    own.start()
    pl.semaphore_wait(barrier, 3 + has_up.astype(jnp.int32) + has_down.astype(jnp.int32))

    pl.when(has_up)(lambda: z_up(0, f_ref).start())
    pl.when(has_down)(lambda: z_down(0, f_ref).start())
    x_copy(z, 0, f_ref).start()
    x_copy(z, 1, f_ref).start()
    cross(0, z, f_ref).start()

    def along_z(d, carry):
        @pl.when(z - d >= 0)
        def _():
            zz = z - d
            z_up_arrival = remote(
                out_ref.at[slot(x, zz)], out_ref.at[slot(x, zz)], zu_s.at[d - 1], zu_r.at[d - 1], other
            )
            z_up_arrival.wait_recv()
            pl.when(has_up)(lambda: z_up(d).start())
            x_copy(zz, 0).start()
            x_copy(zz, 1).start()
            cross(0, zz).start()

        @pl.when(z + d < NZ)
        def _():
            zz = z + d
            z_down_arrival = remote(
                out_ref.at[slot(x, zz)], out_ref.at[slot(x, zz)], zd_s.at[d - 1], zd_r.at[d - 1], other
            )
            z_down_arrival.wait_recv()
            pl.when(has_down)(lambda: z_down(d).start())
            x_copy(zz, 0).start()
            x_copy(zz, 1).start()
            cross(0, zz).start()

        return carry

    lax.fori_loop(1, NZ, along_z, 0)

    def along_x(zz):
        x_arrival(zz, 0).wait_recv()
        x_forward(zz, 0).start()
        cross(NX - 1, zz).start()
        x_arrival(zz, 1).wait_recv()
        x_forward(zz, 1).start()
        cross(1, zz).start()

    along_x(z)

    def along_x_step(d, carry):
        pl.when(z - d >= 0)(lambda: along_x(z - d))
        pl.when(z + d < NZ)(lambda: along_x(z + d))
        return carry

    lax.fori_loop(1, NZ, along_x_step, 0)

    def last_halves(zz):
        f_arrival(zz, 0).wait_recv()
        f_arrival(zz, 1).wait_recv()
        cross(2, zz).start()

    last_halves(z)

    def last_step(d, carry):
        pl.when(z - d >= 0)(lambda: last_halves(z - d))
        pl.when(z + d < NZ)(lambda: last_halves(z + d))
        return carry

    lax.fori_loop(1, NZ, last_step, 0)

    def drain(zz, carry):
        for dx in range(NX):
            cross_arrival(dx, zz).wait_recv()
            cross(dx, zz).wait_send()
        for way in range(2):
            x_copy(zz, way).wait_send()
            x_forward(zz, way).wait_send()
        pl.when(jnp.logical_and(has_up, zz <= z))(lambda: z_up(zz).wait_send())
        pl.when(jnp.logical_and(has_down, zz <= NZ - 1 - z))(lambda: z_down(zz).wait_send())
        return carry

    lax.fori_loop(0, NZ, drain, 0)
    own.wait()


def gather_features(features):
    rows, width = features.shape
    devices = NX * NZ * NC
    dma = pltpu.SemaphoreType.DMA
    return pl.pallas_call(
        gather_kernel,
        out_shape=jax.ShapeDtypeStruct((devices, rows, width), features.dtype),
        in_specs=[pl.BlockSpec(memory_space=pl.ANY)],
        out_specs=pl.BlockSpec(memory_space=pl.ANY),
        scratch_shapes=[dma]
        + [dma((NZ,))] * 4
        + [dma((2, NZ))] * 4
        + [dma((NX, NZ))] * 2,
        compiler_params=pltpu.CompilerParams(collective_id=0, has_side_effects=True),
        name="gather_features",
    )(features)


def multiply_kernel(coords_ref, counts_ref, adj_ref, feat_ref, out_ref, adj_v, feat_v, adj_sem, feat_sem):
    turns = counts_ref[lax.axis_index("row"), lax.axis_index("col")] // GROUP
    feat = pltpu.make_async_copy(feat_ref, feat_v, feat_sem)
    feat.start()

    def adj(g):
        slots = pl.ds(g * GROUP, GROUP)
        return pltpu.make_async_copy(adj_ref.at[slots], adj_v.at[slots], adj_sem.at[g])

    def fetch(g, carry):
        adj(g).start()
        return carry

    lax.fori_loop(0, turns, fetch, 0)
    out_ref[...] = jnp.zeros_like(out_ref)
    feat.wait()

    def turn(g, carry):
        adj(g).wait()
        products = []
        for i in range(GROUP):
            s = g * GROUP + i
            products.append(
                jnp.dot(adj_v[s], feat_v[coords_ref[1, s]], preferred_element_type=jnp.float32)
            )
        for i in range(GROUP):
            out_ref[coords_ref[0, g * GROUP + i]] += products[i]
        return carry

    lax.fori_loop(0, turns, turn, 0)


def multiply_blocks(tile_coords, counts, tile_blocks, feature_blocks, row_blocks):
    slots, block, _ = tile_blocks.shape
    width = feature_blocks.shape[-1]
    dma = pltpu.SemaphoreType.DMA
    return pl.pallas_call(
        multiply_kernel,
        out_shape=jax.ShapeDtypeStruct((row_blocks, block, width), jnp.float32),
        in_specs=[pl.BlockSpec(memory_space=pltpu.SMEM)] * 2 + [pl.BlockSpec(memory_space=pl.ANY)] * 2,
        out_specs=pl.BlockSpec(memory_space=pltpu.VMEM),
        scratch_shapes=[
            pltpu.VMEM(tile_blocks.shape, tile_blocks.dtype),
            pltpu.VMEM(feature_blocks.shape, feature_blocks.dtype),
            dma((slots // GROUP,)),
            dma,
        ],
        compiler_params=pltpu.CompilerParams(vmem_limit_bytes=24 << 20),
        name="multiply_blocks",
    )(tile_coords, counts, tile_blocks, feature_blocks)


def silu_slope(preact, sigmoid_value):
    return sigmoid_value * (1.0 + preact * (1.0 - sigmoid_value))


def layer_kernel(
    p_ref, w_ref, cot_ref, act_ref, grad_ref,
    ysend, yrecv, zsend, zrecv, own_ref, rounded_ref, grad_v, r1, c1, r2, c2, r3, c3, r4,
    ys_s, ys_r, zs_s, zs_r, g_s, g_r,
):
    rows = cot_ref.shape[0]
    half = rows // 2
    members = NX * NY * NC
    r, c = lax.axis_index("row"), lax.axis_index("col")
    x, z, core = r // (NZ * NC), (r // NC) % NZ, r % NC
    y, h = c // NH, c % NH
    me = (x * NY + y) * NC + core

    def member(m):
        return {"row": ((m // (NY * NC)) * NZ + z) * NC + m % NC, "col": ((m // NC) % NY) * NH + h}

    def z_peer(zz):
        return {"row": (x * NZ + zz) * NC + core, "col": c}

    def h_peer(hh):
        return {"row": r, "col": y * NH + hh % NH}

    barrier = pltpu.get_barrier_semaphore()

    def greet(j, carry):
        pl.semaphore_signal(barrier, inc=1, device_id=member((me + j) % members), device_id_type=MESH)
        return carry

    lax.fori_loop(1, members, greet, 0)
    for j in range(1, NZ):
        pl.semaphore_signal(barrier, inc=1, device_id=z_peer((z + j) % NZ), device_id_type=MESH)
    for j in range(1, NH):
        pl.semaphore_signal(barrier, inc=1, device_id=h_peer(h + j), device_id_type=MESH)

    def part(dy, k, b):
        start = (((y + dy) % NY) * NH + (h + k) % NH) * rows + b * half
        return p_ref[pl.ds(pl.multiple_of(start, half), half), :]

    def y_copy(k, i):
        yy = (y + (1 if i % 2 == 0 else NY - 1)) % NY
        return remote(
            ysend.at[k, i], yrecv.at[k, i], ys_s.at[k, i], ys_r.at[k, i], {"row": r, "col": yy * NH + h}
        )

    def z_copy(i):
        return remote(
            zsend.at[i], zrecv.at[i], zs_s.at[i], zs_r.at[i], h_peer(h + (1 if i % 2 == 0 else NH - 1))
        )

    def y_fill(k, i):
        s, w = i // 2, i % 2
        dy = 2 if s == 0 else (1 if w == 0 else -1)
        b = w if s != 1 else 1 - w
        value = part(dy, k, b)
        if s == 2:
            value = value + yrecv[k, w].astype(jnp.float32)
        ysend[k, i] = value.astype(ysend.dtype)

    def y_middle(k):
        for w in range(2):
            y_copy(k, w).wait_recv()
            y_fill(k, 4 + w)
            y_copy(k, 4 + w).start()

    def y_sum(k, b):
        first, second = (4, 3) if b == 0 else (2, 5)
        return part(0, k, b) + yrecv[k, first].astype(jnp.float32) + yrecv[k, second].astype(jnp.float32)

    def y_end(k):
        for i in range(2, 6):
            y_copy(k, i).wait_recv()

    def z_start(i, value):
        zsend[i] = value.astype(zsend.dtype)
        z_copy(i).start()

    def y_launch(k):
        for i in range(4):
            y_copy(k, i).start()

    for i in range(4):
        y_fill(2, i)
    pl.semaphore_wait(barrier, members - 1 + NZ - 1 + NH - 1)
    y_launch(2)
    for i in range(4):
        y_fill(1, i)
    y_launch(1)
    for k in (3, 0):
        for i in range(4):
            y_fill(k, i)
    y_middle(2)
    y_launch(3)
    y_middle(1)
    y_end(2)
    z_start(0, y_sum(2, 0))
    z_start(1, y_sum(2, 1))
    y_launch(0)
    y_middle(3)
    y_end(1)
    z_start(2, y_sum(1, 1))
    y_middle(0)
    y_end(3)
    z_start(3, y_sum(3, 0))
    z_copy(0).wait_recv()
    z_start(4, y_sum(1, 0) + zrecv[0].astype(jnp.float32))
    z_copy(1).wait_recv()
    z_start(5, y_sum(3, 1) + zrecv[1].astype(jnp.float32))
    y_end(0)
    own_ref[0] = y_sum(0, 0)
    own_ref[1] = y_sum(0, 1)
    z_copy(2).wait_recv()
    z_copy(3).wait_recv()
    z_copy(4).wait_recv()
    z_copy(5).wait_recv()
    for b, (first, second) in enumerate(((4, 3), (2, 5))):
        total = own_ref[b] + zrecv[first].astype(jnp.float32) + zrecv[second].astype(jnp.float32)
        rounded_ref[pl.ds(b * half, half), :] = total.astype(rounded_ref.dtype)

    rounded = rounded_ref[...]
    preact = jnp.dot(rounded, w_ref[...], preferred_element_type=jnp.float32)
    sigmoid_value = 1.0 / (1.0 + jnp.exp(-preact))
    act_ref[...] = (preact * sigmoid_value).astype(act_ref.dtype)
    slope_grad = (cot_ref[...].astype(jnp.float32) * silu_slope(preact, sigmoid_value)).astype(jnp.bfloat16)
    local_grad = lax.dot_general(
        rounded, slope_grad, (((0,), (0,)), ((), ())), preferred_element_type=jnp.float32
    )
    lanes = grad_v.shape[-1]
    pieces = local_grad.shape[1] // lanes
    per = members // pieces
    for i in range(pieces):
        grad_v[i * per : (i + 1) * per] = local_grad[:, i * lanes : (i + 1) * lanes].reshape(
            (per,) + grad_v.shape[1:]
        )

    def scatter(j, carry):
        m = (me + j) % members
        remote(grad_v.at[m], r1.at[j - 1], g_s.at[0], g_r.at[0], member(m)).start()
        return carry

    lax.fori_loop(1, members, scatter, 0)
    remote(r1, r1, g_s.at[0], g_r.at[0], member(me)).wait_recv()
    c1[...] = grad_v[me] + jnp.sum(r1[...], axis=0)
    for j in range(1, NZ):
        remote(c1, r2.at[z], g_s.at[1], g_r.at[1], z_peer((z + j) % NZ)).start()
    r2[z] = c1[...]
    remote(r1.at[: NZ - 1], r1.at[: NZ - 1], g_s.at[1], g_r.at[1], member(me)).wait_recv()
    c2[...] = jnp.sum(r2[...], axis=0)
    for j in range(1, NH):
        remote(c2, r3.at[h], g_s.at[2], g_r.at[2], h_peer(h + j)).start()
    r3[h] = c2[...]
    remote(r1.at[: NH - 1], r1.at[: NH - 1], g_s.at[2], g_r.at[2], member(me)).wait_recv()
    c3[...] = jnp.sum(r3[...], axis=0)

    def hand_out(j, carry):
        remote(c3, r4.at[me], g_s.at[3], g_r.at[3], member((me + j) % members)).start()
        return carry

    lax.fori_loop(1, members, hand_out, 0)
    r4[me] = c3[...]
    for k in range(NH):
        for i in range(6):
            y_copy(k, i).wait_send()
    for i in range(6):
        z_copy(i).wait_send()
    remote(r1, r1, g_s.at[0], g_r.at[0], member(me)).wait_send()
    remote(r1.at[: NZ - 1], r1.at[: NZ - 1], g_s.at[1], g_r.at[1], member(me)).wait_send()
    remote(r1.at[: NH - 1], r1.at[: NH - 1], g_s.at[2], g_r.at[2], member(me)).wait_send()
    remote(r1, r1, g_s.at[3], g_r.at[3], member(me)).wait_recv()
    remote(r1, r1, g_s.at[3], g_r.at[3], member(me)).wait_send()
    for i in range(pieces):
        grad_ref[:, i * lanes : (i + 1) * lanes] = r4[i * per : (i + 1) * per].reshape(grad_ref.shape[0], lanes)


def layer(partial_rows, weight, cotangent):
    rows, hidden = cotangent.shape
    width = weight.shape[0]
    half = rows // 2
    members = NX * NY * NC
    lanes = 128
    chunk = (width * hidden // members // lanes, lanes)
    dma = pltpu.SemaphoreType.DMA
    f32, bf16 = jnp.float32, jnp.bfloat16
    vmem = pl.BlockSpec(memory_space=pltpu.VMEM)
    return pl.pallas_call(
        layer_kernel,
        out_shape=(
            jax.ShapeDtypeStruct((rows, hidden), bf16),
            jax.ShapeDtypeStruct((width, hidden), f32),
        ),
        in_specs=[vmem] * 3,
        out_specs=(vmem, vmem),
        scratch_shapes=[
            pltpu.VMEM((NH, 6, half, width), bf16),
            pltpu.VMEM((NH, 6, half, width), bf16),
            pltpu.VMEM((6, half, width), bf16),
            pltpu.VMEM((6, half, width), bf16),
            pltpu.VMEM((2, half, width), f32),
            pltpu.VMEM((rows, width), bf16),
            pltpu.VMEM((members,) + chunk, f32),
            pltpu.VMEM((members - 1,) + chunk, f32),
            pltpu.VMEM(chunk, f32),
            pltpu.VMEM((NZ,) + chunk, f32),
            pltpu.VMEM(chunk, f32),
            pltpu.VMEM((NH,) + chunk, f32),
            pltpu.VMEM(chunk, f32),
            pltpu.VMEM((members,) + chunk, f32),
            dma((NH, 6)),
            dma((NH, 6)),
            dma((6,)),
            dma((6,)),
            dma((4,)),
            dma((4,)),
        ],
        compiler_params=pltpu.CompilerParams(
            collective_id=1, has_side_effects=True, vmem_limit_bytes=24 << 20
        ),
        name="layer",
    )(partial_rows, weight, cotangent)


def body(features, adj_blocks, block_coords, counts, weight, cotangent):
    tile_blocks, tile_coords = adj_blocks[0, 0], block_coords[0, 0]
    block, width = tile_blocks.shape[1], features.shape[1]
    gathered = gather_features(features)
    feature_blocks = gathered.reshape(-1, block, width)
    row_blocks = cotangent.shape[0] * NY * NH // block
    partial_rows = multiply_blocks(tile_coords, counts, tile_blocks, feature_blocks, row_blocks)
    return layer(partial_rows.reshape(row_blocks * block, width), weight, cotangent)


def solution(mesh):
    return jax.shard_map(
        body,
        mesh=mesh,
        in_specs=(
            P(("col", "row"), None),
            P("row", "col", None, None, None),
            P("row", "col", None, None),
            P(),
            P(),
            P(("row", "col"), None),
        ),
        out_specs=(P(("row", "col"), None), P()),
        check_vma=False,
    )
```

```python
import jax
import jax.numpy as jnp
from jax import lax
from jax.experimental import pallas as pl
from jax.experimental.pallas import tpu as pltpu
from jax.sharding import PartitionSpec as P

NX, NZ, NC = 4, 8, 2
NY, NH = 4, 4
UNROLL = 4
NEAR = 4
LAG = 2
MESH = pl.DeviceIdType.MESH


def remote(src, dst, send_sem, recv_sem, device):
    return pltpu.make_async_remote_copy(
        src_ref=src, dst_ref=dst, send_sem=send_sem, recv_sem=recv_sem, device_id=device, device_id_type=MESH
    )


def find_links(coords_ref, live, plan_ref):
    slots = coords_ref.shape[1]
    wide = plan_ref.shape[1]
    rows = jnp.broadcast_to(coords_ref[0:1, :], (slots, slots))
    down = lax.broadcasted_iota(jnp.int32, (slots, slots), 0)
    across = lax.broadcasted_iota(jnp.int32, (slots, slots), 1)
    row_of = jnp.sum(jnp.where(down == across, rows, 0), axis=1, keepdims=True)
    earlier = jnp.logical_and(row_of == rows, down < across)
    before = jnp.max(jnp.where(earlier, down, -1), axis=0, keepdims=True)
    plan_ref[...] = jnp.full(plan_ref.shape, slots, jnp.int32)
    plan_ref[0:1, 0:slots] = jnp.where(before < 0, slots, before)
    place = lax.broadcasted_iota(jnp.int32, (slots, wide), 1)
    slot = lax.broadcasted_iota(jnp.int32, (slots, wide), 0)
    named = jnp.logical_and(row_of == place, slot < live)
    last = jnp.max(jnp.where(named, slot, -1), axis=0, keepdims=True)
    plan_ref[1:2, :] = jnp.where(last < 0, slots, last)


def gather_kernel(
    f_ref, coords_ref, counts_ref, out_ref, plan_ref,
    own_sem, zu_s, zu_r, zd_s, zd_r, xs_s, xs_r, xf_s, xf_r, cc_s, cc_r,
):
    half = f_ref.shape[0] // 2
    r = lax.axis_index("row")
    x, z, core = r // (NZ * NC), (r // NC) % NZ, r % NC

    def slot(xx, zz, cc=None):
        return ((xx % NX) * NZ + zz) * NC + (core if cc is None else cc)

    up, down = {"row": slot(x, z + 1)}, {"row": slot(x, z - 1)}
    right, left = {"row": slot(x + 1, z)}, {"row": slot(x - 1, z)}
    other = {"row": slot(x, z, 1 - core)}

    def send(s, b, send_sem, recv_sem, device, src=None):
        rows = pl.ds(b * half, half)
        there = out_ref.at[s, rows]
        return remote(there if src is None else src.at[rows], there, send_sem, recv_sem, device)

    def z_up(d, b, src=None):
        return send(slot(x, z - d), b, zu_s.at[d, b], zu_r.at[d, b], up, src)

    def z_down(d, b, src=None):
        return send(slot(x, z + d), b, zd_s.at[d, b], zd_r.at[d, b], down, src)

    def z_up_arrival(d, b):
        return send(slot(x, z - d), b, zu_s.at[d - 1, b], zu_r.at[d - 1, b], up)

    def z_down_arrival(d, b):
        return send(slot(x, z + d), b, zd_s.at[d - 1, b], zd_r.at[d - 1, b], down)

    def x_copy(zz, way, b, src=None):
        return send(
            slot(x, zz), b, xs_s.at[way, zz, b], xs_r.at[way, zz, b], right if way == 0 else left, src
        )

    def x_arrival(zz, way, b):
        s = slot(x - 1 if way == 0 else x + 1, zz)
        return send(s, b, xs_s.at[way, zz, b], xs_r.at[way, zz, b], right)

    def x_forward(zz, way):
        s = slot(x - 1 if way == 0 else x + 1, zz)
        return send(s, way, xf_s.at[way, zz], xf_r.at[way, zz], right if way == 0 else left)

    def f_arrival(zz, way):
        return send(slot(x + 2, zz), way, xf_s.at[way, zz], xf_r.at[way, zz], right)

    def cross(dx, zz, src=None):
        there = out_ref.at[slot(x + dx, zz)]
        return remote(there if src is None else src, there, cc_s.at[dx, zz], cc_r.at[dx, zz], other)

    def cross_arrival(dx, zz):
        here = out_ref.at[slot(x + dx, zz, 1 - core)]
        return remote(here, here, cc_s.at[dx, zz], cc_r.at[dx, zz], other)

    has_up, has_down = z < NZ - 1, z > 0
    barrier = pltpu.get_barrier_semaphore()
    for device in (right, left, other):
        pl.semaphore_signal(barrier, inc=1, device_id=device, device_id_type=MESH)

    @pl.when(has_up)
    def _():
        pl.semaphore_signal(barrier, inc=1, device_id=up, device_id_type=MESH)

    @pl.when(has_down)
    def _():
        pl.semaphore_signal(barrier, inc=1, device_id=down, device_id_type=MESH)

    own = pltpu.make_async_copy(f_ref, out_ref.at[r], own_sem)
    own.start()
    pl.semaphore_wait(barrier, 3 + has_up.astype(jnp.int32) + has_down.astype(jnp.int32))

    for b in range(2):
        pl.when(has_up)(lambda b=b: z_up(0, b, f_ref).start())
        pl.when(has_down)(lambda b=b: z_down(0, b, f_ref).start())
        x_copy(z, 0, b, f_ref).start()
        x_copy(z, 1, 1 - b, f_ref).start()
    cross(0, z, f_ref).start()
    find_links(coords_ref, counts_ref[r, lax.axis_index("col")], plan_ref)

    def along_z(d):
        below, above = z - d >= 0, z + d < NZ
        for b in range(2):

            @pl.when(below)
            def _():
                z_up_arrival(d, b).wait_recv()
                pl.when(has_up)(lambda: z_up(d, b).start())
                x_copy(z - d, 0, b).start()
                x_copy(z - d, 1, b).start()

            @pl.when(above)
            def _():
                z_down_arrival(d, b).wait_recv()
                pl.when(has_down)(lambda: z_down(d, b).start())
                x_copy(z + d, 0, b).start()
                x_copy(z + d, 1, b).start()

        pl.when(below)(lambda: cross(0, z - d).start())
        pl.when(above)(lambda: cross(0, z + d).start())

    def along_x(zz):
        for way in range(2):
            x_arrival(zz, way, way).wait_recv()
            x_forward(zz, way).start()
        x_arrival(zz, 0, 1).wait_recv()
        cross(NX - 1, zz).start()
        x_arrival(zz, 1, 0).wait_recv()
        cross(1, zz).start()

    def last_halves(zz):
        f_arrival(zz, 0).wait_recv()
        f_arrival(zz, 1).wait_recv()
        cross(2, zz).start()

    def at_distance(d, act):
        pl.when(z - d >= 0)(lambda: act(z - d))
        pl.when(jnp.logical_and(d > 0, z + d < NZ))(lambda: act(z + d))

    def first_steps(d, carry):
        along_z(d)
        return carry

    def steps(d, carry):
        along_z(d)
        at_distance(d - LAG, along_x)
        return carry

    def last_x(d, carry):
        at_distance(d, along_x)
        return carry

    def last_steps(d, carry):
        at_distance(d, last_halves)
        return carry

    lax.fori_loop(1, LAG, first_steps, 0)
    lax.fori_loop(LAG, NZ, steps, 0)
    lax.fori_loop(NZ - LAG, NZ, last_x, 0)
    lax.fori_loop(0, NZ, last_steps, 0)

    def drain(zz, carry):
        for dx in range(NX):
            cross_arrival(dx, zz).wait_recv()
            cross(dx, zz).wait_send()
        for way in range(2):
            x_forward(zz, way).wait_send()
        for b in range(2):
            x_copy(zz, 0, b).wait_send()
            x_copy(zz, 1, b).wait_send()
            pl.when(jnp.logical_and(has_up, zz <= z))(lambda b=b: z_up(zz, b).wait_send())
            pl.when(jnp.logical_and(has_down, zz <= NZ - 1 - z))(lambda b=b: z_down(zz, b).wait_send())
        return carry

    lax.fori_loop(0, NZ, drain, 0)
    own.wait()


def gather_features(features, tile_coords, counts):
    rows, width = features.shape
    devices = NX * NZ * NC
    dma = pltpu.SemaphoreType.DMA
    vmem = pl.BlockSpec(memory_space=pltpu.VMEM)
    return pl.pallas_call(
        gather_kernel,
        out_shape=(
            jax.ShapeDtypeStruct((devices, rows, width), features.dtype),
            jax.ShapeDtypeStruct((2, 128), jnp.int32),
        ),
        in_specs=[pl.BlockSpec(memory_space=pl.ANY), vmem, pl.BlockSpec(memory_space=pltpu.SMEM)],
        out_specs=(pl.BlockSpec(memory_space=pl.ANY), vmem),
        scratch_shapes=[dma]
        + [dma((NZ, 2))] * 4
        + [dma((2, NZ, 2))] * 2
        + [dma((2, NZ))] * 2
        + [dma((NX, NZ))] * 2,
        compiler_params=pltpu.CompilerParams(
            collective_id=0, has_side_effects=True, vmem_limit_bytes=48 << 20
        ),
        name="gather_features",
    )(features, tile_coords, counts)


def silu_slope(preact, sigmoid_value):
    return sigmoid_value * (1.0 + preact * (1.0 - sigmoid_value))


def layer_kernel(
    cols_ref, plan_ref, adj_ref, feat_ref, w_ref, cot_ref, act_ref, grad_ref,
    adj_v, feat_v, sums, ysend, yrecv, zsend, zrecv, own_ref, rounded_ref, grad_v, r1, c1, r2, c2, r3, c3, r4,
    in_sem, ys_s, ys_r, zs_s, zs_r, g_s, g_r,
):
    rows = cot_ref.shape[0]
    half = rows // 2
    members = NX * NY * NC
    r, c = lax.axis_index("row"), lax.axis_index("col")
    x, z, core = r // (NZ * NC), (r // NC) % NZ, r % NC
    y, h = c // NH, c % NH
    me = (x * NY + y) * NC + core
    tall = NZ * NH
    far = tall // NEAR
    level = h * NZ + z
    place, team = level % NEAR, level // NEAR
    slots = adj_ref.shape[0]

    adj = pltpu.make_async_copy(adj_ref, adj_v, in_sem.at[0])
    feat = pltpu.make_async_copy(feat_ref, feat_v, in_sem.at[1])
    feat.start()
    adj.start()

    def member(m):
        return {"row": ((m // (NY * NC)) * NZ + z) * NC + m % NC, "col": ((m // NC) % NY) * NH + h}

    def at_level(t):
        return {"row": (x * NZ + t % NZ) * NC + core, "col": y * NH + t // NZ}

    def near_peer(j):
        return at_level(team * NEAR + (place + j) % NEAR)

    def far_peer(j):
        return at_level((level + j * NEAR) % tall)

    def h_peer(hh):
        return {"row": r, "col": y * NH + hh % NH}

    barrier = pltpu.get_barrier_semaphore()

    def greet(j, carry):
        pl.semaphore_signal(barrier, inc=1, device_id=member((me + j) % members), device_id_type=MESH)
        return carry

    lax.fori_loop(1, members, greet, 0)
    for j in range(1, NEAR):
        pl.semaphore_signal(barrier, inc=1, device_id=near_peer(j), device_id_type=MESH)
    for j in range(1, far):
        pl.semaphore_signal(barrier, inc=1, device_id=far_peer(j), device_id_type=MESH)

    sums[slots] = jnp.zeros(sums.shape[1:], sums.dtype)
    feat.wait()
    adj.wait()

    def turn(g, carry):
        first = g * UNROLL
        products = [
            jnp.dot(adj_v[first + i], feat_v[cols_ref[0, first + i]], preferred_element_type=jnp.float32)
            for i in range(UNROLL)
        ]
        for i in range(UNROLL):
            sums[first + i] = products[i] + sums[plan_ref[0, first + i]]
        return carry

    lax.fori_loop(0, slots // UNROLL, turn, 0)

    def part(dy, k, b):
        block_row = (((y + dy) % NY) * NH + (h + k) % NH) * 2 + b
        return sums[plan_ref[1, block_row]]

    def y_copy(k, i):
        yy = (y + (1 if i % 2 == 0 else NY - 1)) % NY
        return remote(
            ysend.at[k, i], yrecv.at[k, i], ys_s.at[k, i], ys_r.at[k, i], {"row": r, "col": yy * NH + h}
        )

    def z_copy(i):
        return remote(
            zsend.at[i], zrecv.at[i], zs_s.at[i], zs_r.at[i], h_peer(h + (1 if i % 2 == 0 else NH - 1))
        )

    def y_fill(k, i):
        s, w = i // 2, i % 2
        dy = 2 if s == 0 else (1 if w == 0 else -1)
        b = w if s != 1 else 1 - w
        value = part(dy, k, b)
        if s == 2:
            value = value + yrecv[k, w].astype(jnp.float32)
        ysend[k, i] = value.astype(ysend.dtype)

    def y_middle(k):
        for w in range(2):
            y_copy(k, w).wait_recv()
            y_fill(k, 4 + w)
            y_copy(k, 4 + w).start()

    def y_sum(k, b):
        first, second = (4, 3) if b == 0 else (2, 5)
        return part(0, k, b) + yrecv[k, first].astype(jnp.float32) + yrecv[k, second].astype(jnp.float32)

    def y_end(k):
        for i in range(2, 6):
            y_copy(k, i).wait_recv()

    def z_start(i, value):
        zsend[i] = value.astype(zsend.dtype)
        z_copy(i).start()

    def y_launch(k):
        for i in range(4):
            y_copy(k, i).start()

    for i in range(4):
        y_fill(2, i)
    pl.semaphore_wait(barrier, members - 1 + NEAR - 1 + far - 1)
    y_launch(2)
    for i in range(4):
        y_fill(1, i)
    y_launch(1)
    for k in (3, 0):
        for i in range(4):
            y_fill(k, i)
    y_middle(2)
    y_launch(3)
    y_middle(1)
    y_end(2)
    z_start(0, y_sum(2, 0))
    z_start(1, y_sum(2, 1))
    y_launch(0)
    y_middle(3)
    y_end(1)
    z_start(2, y_sum(1, 1))
    y_middle(0)
    y_end(3)
    z_start(3, y_sum(3, 0))
    z_copy(0).wait_recv()
    z_start(4, y_sum(1, 0) + zrecv[0].astype(jnp.float32))
    z_copy(1).wait_recv()
    z_start(5, y_sum(3, 1) + zrecv[1].astype(jnp.float32))
    y_end(0)
    own_ref[0] = y_sum(0, 0)
    own_ref[1] = y_sum(0, 1)
    z_copy(2).wait_recv()
    z_copy(3).wait_recv()
    z_copy(4).wait_recv()
    z_copy(5).wait_recv()
    for b, (first, second) in enumerate(((4, 3), (2, 5))):
        total = own_ref[b] + zrecv[first].astype(jnp.float32) + zrecv[second].astype(jnp.float32)
        rounded_ref[pl.ds(b * half, half), :] = total.astype(rounded_ref.dtype)

    rounded = rounded_ref[...]
    preact = jnp.dot(rounded, w_ref[...], preferred_element_type=jnp.float32)
    sigmoid_value = 1.0 / (1.0 + jnp.exp(-preact))
    act_ref[...] = (preact * sigmoid_value).astype(act_ref.dtype)
    slope_grad = (cot_ref[...].astype(jnp.float32) * silu_slope(preact, sigmoid_value)).astype(jnp.bfloat16)
    local_grad = lax.dot_general(
        rounded, slope_grad, (((0,), (0,)), ((), ())), preferred_element_type=jnp.float32
    )
    lanes = grad_v.shape[-1]
    pieces = local_grad.shape[1] // lanes
    per = members // pieces
    for i in range(pieces):
        grad_v[i * per : (i + 1) * per] = local_grad[:, i * lanes : (i + 1) * lanes].reshape(
            (per,) + grad_v.shape[1:]
        )

    def scatter(j, carry):
        m = (me + j) % members
        remote(grad_v.at[m], r1.at[j - 1], g_s.at[0], g_r.at[0], member(m)).start()
        return carry

    lax.fori_loop(1, members, scatter, 0)
    remote(r1, r1, g_s.at[0], g_r.at[0], member(me)).wait_recv()
    c1[...] = grad_v[me] + jnp.sum(r1[...], axis=0)
    for j in range(1, NEAR):
        remote(c1, r2.at[place], g_s.at[1], g_r.at[1], near_peer(j)).start()
    r2[place] = c1[...]
    remote(r1.at[: NEAR - 1], r1.at[: NEAR - 1], g_s.at[1], g_r.at[1], member(me)).wait_recv()
    c2[...] = jnp.sum(r2[...], axis=0)
    for j in range(1, far):
        remote(c2, r3.at[team], g_s.at[2], g_r.at[2], far_peer(far - j)).start()
    r3[team] = c2[...]
    remote(r1.at[: far - 1], r1.at[: far - 1], g_s.at[2], g_r.at[2], member(me)).wait_recv()
    c3[...] = jnp.sum(r3[...], axis=0)

    def hand_out(j, carry):
        remote(c3, r4.at[me], g_s.at[3], g_r.at[3], member((me + j) % members)).start()
        return carry

    lax.fori_loop(1, members, hand_out, 0)
    r4[me] = c3[...]
    for k in range(NH):
        for i in range(6):
            y_copy(k, i).wait_send()
    for i in range(6):
        z_copy(i).wait_send()
    remote(r1, r1, g_s.at[0], g_r.at[0], member(me)).wait_send()
    remote(r1.at[: NEAR - 1], r1.at[: NEAR - 1], g_s.at[1], g_r.at[1], member(me)).wait_send()
    remote(r1.at[: far - 1], r1.at[: far - 1], g_s.at[2], g_r.at[2], member(me)).wait_send()
    remote(r1, r1, g_s.at[3], g_r.at[3], member(me)).wait_recv()
    remote(r1, r1, g_s.at[3], g_r.at[3], member(me)).wait_send()
    for i in range(pieces):
        grad_ref[:, i * lanes : (i + 1) * lanes] = r4[i * per : (i + 1) * per].reshape(grad_ref.shape[0], lanes)


def layer(cols, plan, tile_blocks, feature_blocks, weight, cotangent):
    rows, hidden = cotangent.shape
    width = weight.shape[0]
    half = rows // 2
    members = NX * NY * NC
    lanes = 128
    chunk = (width * hidden // members // lanes, lanes)
    dma = pltpu.SemaphoreType.DMA
    f32, bf16 = jnp.float32, jnp.bfloat16
    vmem = pl.BlockSpec(memory_space=pltpu.VMEM)
    smem, hbm = pl.BlockSpec(memory_space=pltpu.SMEM), pl.BlockSpec(memory_space=pl.ANY)
    slots, block, _ = tile_blocks.shape
    return pl.pallas_call(
        layer_kernel,
        out_shape=(
            jax.ShapeDtypeStruct((rows, hidden), bf16),
            jax.ShapeDtypeStruct((width, hidden), f32),
        ),
        in_specs=[smem, smem, hbm, hbm, vmem, vmem],
        out_specs=(vmem, vmem),
        scratch_shapes=[
            pltpu.VMEM(tile_blocks.shape, bf16),
            pltpu.VMEM(feature_blocks.shape, bf16),
            pltpu.VMEM((slots + 1, block, width), f32),
            pltpu.VMEM((NH, 6, half, width), bf16),
            pltpu.VMEM((NH, 6, half, width), bf16),
            pltpu.VMEM((6, half, width), bf16),
            pltpu.VMEM((6, half, width), bf16),
            pltpu.VMEM((2, half, width), f32),
            pltpu.VMEM((rows, width), bf16),
            pltpu.VMEM((members,) + chunk, f32),
            pltpu.VMEM((members - 1,) + chunk, f32),
            pltpu.VMEM(chunk, f32),
            pltpu.VMEM((NEAR,) + chunk, f32),
            pltpu.VMEM(chunk, f32),
            pltpu.VMEM((NZ * NH // NEAR,) + chunk, f32),
            pltpu.VMEM(chunk, f32),
            pltpu.VMEM((members,) + chunk, f32),
            dma((2,)),
            dma((NH, 6)),
            dma((NH, 6)),
            dma((6,)),
            dma((6,)),
            dma((4,)),
            dma((4,)),
        ],
        compiler_params=pltpu.CompilerParams(
            collective_id=1, has_side_effects=True, vmem_limit_bytes=48 << 20
        ),
        name="layer",
    )(cols, plan, tile_blocks, feature_blocks, weight, cotangent)


def body(features, adj_blocks, block_coords, counts, weight, cotangent):
    tile_blocks, tile_coords = adj_blocks[0, 0], block_coords[0, 0]
    block, width = tile_blocks.shape[1], features.shape[1]
    gathered, plan = gather_features(features, tile_coords, counts)
    feature_blocks = gathered.reshape(-1, block, width)
    return layer(tile_coords[1:], plan, tile_blocks, feature_blocks, weight, cotangent)


def solution(mesh):
    return jax.shard_map(
        body,
        mesh=mesh,
        in_specs=(
            P(("col", "row"), None),
            P("row", "col", None, None, None),
            P("row", "col", None, None),
            P(),
            P(),
            P(("row", "col"), None),
        ),
        out_specs=(P(("row", "col"), None), P()),
        check_vma=False,
    )
```

```python
import jax
import jax.numpy as jnp
from jax import lax
from jax.experimental import pallas as pl
from jax.experimental.pallas import tpu as pltpu
from jax.sharding import PartitionSpec as P

NX, NZ, NC = 4, 8, 2
NY, NH = 4, 4
NEAR = 4
UNROLL = 8
MESH = pl.DeviceIdType.MESH
F32, BF16 = jnp.float32, jnp.bfloat16


def remote(src, dst, send_sem, recv_sem, device):
    return pltpu.make_async_remote_copy(
        src_ref=src, dst_ref=dst, send_sem=send_sem, recv_sem=recv_sem, device_id=device, device_id_type=MESH
    )


class Place:
    def __init__(self):
        self.r, self.c = lax.axis_index("row"), lax.axis_index("col")
        self.x, self.z, self.core = self.r // (NZ * NC), (self.r // NC) % NZ, self.r % NC
        self.y, self.h = self.c // NH, self.c % NH
        self.members = NX * NY * NC
        self.me = (self.x * NY + self.y) * NC + self.core
        self.tall = NZ * NH
        self.level = self.h * NZ + self.z
        self.near, self.team = self.level % NEAR, self.level // NEAR

    def slot(self, x, z, core=None):
        return ((x % NX) * NZ + z) * NC + (self.core if core is None else core)

    def in_column(self, x, z, core=None):
        return {"row": self.slot(x, z, core), "col": self.c}

    def member(self, m):
        return {
            "row": ((m // (NY * NC)) * NZ + self.z) * NC + m % NC,
            "col": ((m // NC) % NY) * NH + self.h,
        }

    def at_level(self, t):
        return {"row": (self.x * NZ + t % NZ) * NC + self.core, "col": self.y * NH + t // NZ}

    def up(self, steps):
        return self.at_level((self.level + steps) % self.tall)

    def at_y(self, y):
        return {"row": self.r, "col": (y % NY) * NH + self.h}

    def at_h(self, h):
        return {"row": self.r, "col": self.y * NH + h % NH}

    def offsets(self, steps):
        return sorted({s % self.tall for s in steps} - {0})


def meet(p):
    barrier = pltpu.get_barrier_semaphore()
    near = p.offsets(range(-NEAR, NEAR + 1))
    for s in near:
        pl.semaphore_signal(barrier, inc=1, device_id=p.up(s), device_id_type=MESH)

    def greet(j, carry):
        pl.semaphore_signal(barrier, inc=1, device_id=p.member((p.me + j) % p.members), device_id_type=MESH)
        return carry

    lax.fori_loop(1, p.members, greet, 0)
    pl.semaphore_wait(barrier, p.members - 1 + len(near))


def tell(p, sem, steps):
    for s in p.offsets((-steps, steps)):
        pl.semaphore_signal(sem, inc=1, device_id=p.up(s), device_id_type=MESH)


def hear(p, sem, steps):
    if p.offsets((-steps, steps)):
        pl.semaphore_wait(sem, len(p.offsets((-steps, steps))))


class Gather:
    def __init__(self, p, f_ref, out_ref, zu_s, zu_r, zd_s, zd_r, xs_s, xs_r, xf_s, xf_r, cc_s, cc_r):
        self.p, self.f_ref, self.out_ref = p, f_ref, out_ref
        self.zu_s, self.zu_r, self.zd_s, self.zd_r = zu_s, zu_r, zd_s, zd_r
        self.xs_s, self.xs_r, self.xf_s, self.xf_r, self.cc_s, self.cc_r = xs_s, xs_r, xf_s, xf_r, cc_s, cc_r
        self.has_up, self.has_down = p.z < NZ - 1, p.z > 0
        self.far_up, self.far_down = p.z + NEAR < NZ, p.z - NEAR >= 0
        self.right, self.left = p.in_column(p.x + 1, p.z), p.in_column(p.x - 1, p.z)
        self.other = p.in_column(p.x, p.z, 1 - p.core)

    def send(self, s, b, send_sem, recv_sem, device, own=False):
        there = self.out_ref.at[2 * s + b]
        return remote(self.f_ref.at[b] if own else there, there, send_sem, recv_sem, device)

    def both(self, s):
        return self.out_ref.at[pl.ds(2 * s, 2)]

    def z_up(self, d, b, own=False, steps=1):
        k = d + steps - 1
        device = self.p.in_column(self.p.x, self.p.z + steps)
        return self.send(self.p.slot(self.p.x, self.p.z - d), b, self.zu_s.at[k, b], self.zu_r.at[k, b], device, own)

    def z_down(self, d, b, own=False, steps=1):
        k = d + steps - 1
        device = self.p.in_column(self.p.x, self.p.z - steps)
        return self.send(self.p.slot(self.p.x, self.p.z + d), b, self.zd_s.at[k, b], self.zd_r.at[k, b], device, own)

    def z_up_arrival(self, d, b):
        s = self.p.slot(self.p.x, self.p.z - d)
        return self.send(s, b, self.zu_s.at[d - 1, b], self.zu_r.at[d - 1, b], self.other)

    def z_down_arrival(self, d, b):
        s = self.p.slot(self.p.x, self.p.z + d)
        return self.send(s, b, self.zd_s.at[d - 1, b], self.zd_r.at[d - 1, b], self.other)

    def x_copy(self, z, way, b, own=False):
        device = self.right if way == 0 else self.left
        return self.send(self.p.slot(self.p.x, z), b, self.xs_s.at[way, z, b], self.xs_r.at[way, z, b], device, own)

    def x_arrival(self, z, way, b):
        s = self.p.slot(self.p.x - 1 if way == 0 else self.p.x + 1, z)
        return self.send(s, b, self.xs_s.at[way, z, b], self.xs_r.at[way, z, b], self.right)

    def x_forward(self, z, way):
        s = self.p.slot(self.p.x - 1 if way == 0 else self.p.x + 1, z)
        device = self.right if way == 0 else self.left
        return self.send(s, way, self.xf_s.at[way, z], self.xf_r.at[way, z], device)

    def f_arrival(self, z, way):
        return self.send(self.p.slot(self.p.x + 2, z), way, self.xf_s.at[way, z], self.xf_r.at[way, z], self.right)

    def cross(self, dx, z, own=False):
        there = self.both(self.p.slot(self.p.x + dx, z))
        return remote(self.f_ref if own else there, there, self.cc_s.at[dx, z], self.cc_r.at[dx, z], self.other)

    def cross_arrival(self, dx, z):
        here = self.both(self.p.slot(self.p.x + dx, z, 1 - self.p.core))
        return remote(here, here, self.cc_s.at[dx, z], self.cc_r.at[dx, z], self.other)

    def begin(self):
        z = self.p.z
        for b in range(2):
            pl.when(self.has_up)(lambda b=b: self.z_up(0, b, True).start())
            pl.when(self.has_down)(lambda b=b: self.z_down(0, b, True).start())
            self.x_copy(z, 0, b, True).start()
            self.x_copy(z, 1, 1 - b, True).start()
            pl.when(self.far_up)(lambda b=b: self.z_up(0, b, True, NEAR).start())
            pl.when(self.far_down)(lambda b=b: self.z_down(0, b, True, NEAR).start())
        self.cross(0, z, True).start()

    def along_z(self, d, use):
        z = self.p.z
        below, above = jnp.logical_and(use, z - d >= 0), jnp.logical_and(use, z + d < NZ)
        on = d != NEAR - 1
        for b in range(2):

            @pl.when(below)
            def _():
                self.z_up_arrival(d, b).wait_recv()
                pl.when(jnp.logical_and(on, self.has_up))(lambda: self.z_up(d, b).start())
                self.x_copy(z - d, 0, b).start()
                self.x_copy(z - d, 1, b).start()

            @pl.when(above)
            def _():
                self.z_down_arrival(d, b).wait_recv()
                pl.when(jnp.logical_and(on, self.has_down))(lambda: self.z_down(d, b).start())
                self.x_copy(z + d, 0, b).start()
                self.x_copy(z + d, 1, b).start()

        pl.when(below)(lambda: self.cross(0, z - d).start())
        pl.when(above)(lambda: self.cross(0, z + d).start())

    def along_x(self, z):
        for way in range(2):
            self.x_arrival(z, way, way).wait_recv()
            self.x_forward(z, way).start()
        self.x_arrival(z, 0, 1).wait_recv()
        self.cross(NX - 1, z).start()
        self.x_arrival(z, 1, 0).wait_recv()
        self.cross(1, z).start()

    def last_halves(self, z):
        self.f_arrival(z, 0).wait_recv()
        self.f_arrival(z, 1).wait_recv()
        self.cross(2, z).start()

    def at_distance(self, d, act, use=True):
        z = self.p.z
        pl.when(jnp.logical_and(use, z - d >= 0))(lambda: act(z - d))
        pl.when(jnp.logical_and(use, jnp.logical_and(d > 0, z + d < NZ)))(lambda: act(z + d))

    def go_on(self, first, end):
        def distance(k):
            return k // 2 + 1 + (NEAR - 1) * (k % 2)

        def step(k, carry):
            self.along_z(distance(k), k != NZ - 2)
            pl.when(k == 1)(lambda: self.along_x(self.p.z))
            self.at_distance(distance(k - 2), self.along_x, k >= 2)
            return carry

        lax.fori_loop(first, end, step, 0)

    def finish(self):
        self.at_distance(NZ - 1, self.along_x)

        def last(d, carry):
            self.at_distance(d, self.last_halves)
            return carry

        lax.fori_loop(0, NZ, last, 0)

        def arrivals(z, carry):
            for dx in range(NX):
                self.cross_arrival(dx, z).wait_recv()
            return carry

        lax.fori_loop(0, NZ, arrivals, 0)

    def drain(self):
        z = self.p.z

        def sent(k, carry):
            for dx in range(NX):
                self.cross(dx, k).wait_send()
            for way in range(2):
                self.x_forward(k, way).wait_send()
                for b in range(2):
                    self.x_copy(k, way, b).wait_send()
            on = jnp.logical_and(k != NEAR - 1, jnp.logical_and(self.has_up, k <= z))
            back = jnp.logical_and(k != NEAR - 1, jnp.logical_and(self.has_down, k <= NZ - 1 - z))
            for b in range(2):
                pl.when(on)(lambda b=b: self.z_up(k, b).wait_send())
                pl.when(back)(lambda b=b: self.z_down(k, b).wait_send())
            return carry

        lax.fori_loop(0, NZ, sent, 0)
        for b in range(2):
            pl.when(self.far_up)(lambda b=b: self.z_up(0, b, True, NEAR).wait_send())
            pl.when(self.far_down)(lambda b=b: self.z_down(0, b, True, NEAR).wait_send())


def find_links(coords, live, plan_ref):
    slots, wide = coords.shape[1], plan_ref.shape[1]
    rows = jnp.broadcast_to(coords[0:1, :], (slots, slots))
    down = lax.broadcasted_iota(jnp.int32, (slots, slots), 0)
    across = lax.broadcasted_iota(jnp.int32, (slots, slots), 1)
    row_of = jnp.sum(jnp.where(down == across, rows, 0), axis=1, keepdims=True)
    earlier = jnp.logical_and(row_of == rows, down < across)
    before = jnp.max(jnp.where(earlier, down, -1), axis=0, keepdims=True)
    plan_ref[...] = jnp.full(plan_ref.shape, slots, jnp.int32)
    plan_ref[0:1, 0:slots] = jnp.where(before < 0, slots, before)
    place = lax.broadcasted_iota(jnp.int32, (slots, wide), 1)
    slot = lax.broadcasted_iota(jnp.int32, (slots, wide), 0)
    named = jnp.logical_and(row_of == place, slot < live)
    last = jnp.max(jnp.where(named, slot, -1), axis=0, keepdims=True)
    plan_ref[1:2, :] = jnp.where(last < 0, slots, last)


def multiply(coords, plan, adj_v, feat_v, sums):
    def turn(g, carry):
        first = g * UNROLL
        products = [
            jnp.dot(adj_v[first + i], feat_v[coords[1, first + i]], preferred_element_type=F32)
            for i in range(UNROLL)
        ]
        for i in range(UNROLL):
            sums[first + i] = products[i] + sums[plan[0, first + i]]
        return carry

    lax.fori_loop(0, adj_v.shape[0] // UNROLL, turn, 0)


def reduce_rows(p, plan, sums, ysend, yrecv, zsend, zrecv, own_ref, ys_s, ys_r, zs_s, zs_r):
    half = sums.shape[1]

    def part(dy, k, b):
        block_row = (((p.y + dy) % NY) * NH + (p.h + k) % NH) * 2 + b
        return sums[plan[1, block_row]]

    def y_copy(k, dy):
        i = dy - 1
        return remote(ysend.at[k, i], yrecv.at[k, i], ys_s.at[k, i], ys_r.at[k, i], p.at_y(p.y + dy))

    def y_start(k):
        for dy in (2, 1, 3):
            for b in range(2):
                ysend[k, dy - 1, pl.ds(b * half, half)] = part(dy, k, b).astype(BF16)
            y_copy(k, dy).start()

    def y_end(k):
        for dy in range(1, NY):
            y_copy(k, dy).wait_recv()

    def y_sum(k, b):
        total = part(0, k, b)
        for i in range(NY - 1):
            total = total + yrecv[k, i, pl.ds(b * half, half)].astype(F32)
        return total

    def z_copy(i):
        device = p.at_h(p.h + (1 if i % 2 == 0 else NH - 1))
        return remote(zsend.at[i], zrecv.at[i], zs_s.at[i], zs_r.at[i], device)

    def z_start(i, value):
        zsend[i] = value.astype(BF16)
        z_copy(i).start()

    for k in (2, 1, 3, 0):
        y_start(k)
    y_end(2)
    z_start(0, y_sum(2, 0))
    z_start(1, y_sum(2, 1))
    y_end(1)
    z_start(2, y_sum(1, 1))
    y_end(3)
    z_start(3, y_sum(3, 0))
    own_ref[0] = y_sum(1, 0)
    own_ref[1] = y_sum(3, 1)
    z_copy(0).wait_recv()
    z_start(4, own_ref[0] + zrecv[0].astype(F32))
    z_copy(1).wait_recv()
    z_start(5, own_ref[1] + zrecv[1].astype(F32))
    y_end(0)
    own_ref[0] = y_sum(0, 0)
    own_ref[1] = y_sum(0, 1)

    def drain():
        for k in range(NH):
            for dy in range(1, NY):
                y_copy(k, dy).wait_send()
        for i in range(6):
            z_copy(i).wait_send()

    def total(b):
        first, second = ((3, 4), (2, 5))[b]
        z_copy(first).wait_recv()
        z_copy(second).wait_recv()
        return own_ref[b] + zrecv[first].astype(F32) + zrecv[second].astype(F32)

    return total, drain


def silu_slope(preact, sigmoid_value):
    return sigmoid_value * (1.0 + preact * (1.0 - sigmoid_value))


def apply_layer(rounded, weight, cotangent, act_ref, grad_v):
    preact = jnp.dot(rounded, weight, preferred_element_type=F32)
    sigmoid_value = 1.0 / (1.0 + jnp.exp(-preact))
    act_ref[...] = (preact * sigmoid_value).astype(BF16)
    slope_grad = (cotangent.astype(F32) * silu_slope(preact, sigmoid_value)).astype(BF16)
    local_grad = lax.dot_general(rounded, slope_grad, (((0,), (0,)), ((), ())), preferred_element_type=F32)
    members, chunk, lanes = grad_v.shape
    per = members * lanes // local_grad.shape[1]
    for i in range(members // per):
        grad_v[i * per : (i + 1) * per] = local_grad[:, i * lanes : (i + 1) * lanes].reshape(per, chunk, lanes)


def sum_gradient(p, grad_v, r1, c1, r2, c2, r3, c3, r4, g_s, g_r, meanwhile):
    far = p.tall // NEAR

    def all_of(count, k):
        return remote(r1.at[:count], r1.at[:count], g_s.at[k], g_r.at[k], p.member(p.me))

    def scatter(j, carry):
        m = (p.me + j) % p.members
        remote(grad_v.at[m], r1.at[j - 1], g_s.at[0], g_r.at[0], p.member(m)).start()
        return carry

    lax.fori_loop(1, p.members, scatter, 0)
    all_of(p.members - 1, 0).wait_recv()
    c1[...] = grad_v[p.me] + jnp.sum(r1[...], axis=0)
    for j in range(1, NEAR):
        there = p.at_level(p.team * NEAR + (p.near + j) % NEAR)
        remote(c1, r2.at[p.near], g_s.at[1], g_r.at[1], there).start()
    r2[p.near] = c1[...]
    all_of(NEAR - 1, 1).wait_recv()
    c2[...] = jnp.sum(r2[...], axis=0)
    for j in sorted(range(1, far), key=lambda j: -min(j, far - j)):
        remote(c2, r3.at[p.team], g_s.at[2], g_r.at[2], p.up(j * NEAR)).start()
    r3[p.team] = c2[...]
    meanwhile()
    all_of(p.members - 1, 0).wait_send()
    all_of(NEAR - 1, 1).wait_send()
    all_of(far - 1, 2).wait_recv()
    c3[...] = jnp.sum(r3[...], axis=0)

    def hand_out(j, carry):
        remote(c3, r4.at[p.me], g_s.at[3], g_r.at[3], p.member((p.me + j) % p.members)).start()
        return carry

    lax.fori_loop(1, p.members, hand_out, 0)
    r4[p.me] = c3[...]
    all_of(far - 1, 2).wait_send()
    all_of(p.members - 1, 3).wait_recv()
    all_of(p.members - 1, 3).wait_send()


def write_gradient(r4, grad_ref):
    members, chunk, lanes = r4.shape
    per = grad_ref.shape[0] // chunk
    for i in range(members // per):
        grad_ref[:, i * lanes : (i + 1) * lanes] = r4[i * per : (i + 1) * per].reshape(per * chunk, lanes)


def gather_scratch(rows, width):
    dma = pltpu.SemaphoreType.DMA
    return (
        [pltpu.VMEM((2 * NX * NZ * NC, rows // 2, width), BF16)]
        + [dma((NZ, 2))] * 4
        + [dma((2, NZ, 2))] * 2
        + [dma((2, NZ))] * 2
        + [dma((NX, NZ))] * 2
    )


def reduce_scratch(rows, width):
    dma = pltpu.SemaphoreType.DMA
    half = rows // 2
    return (
        [pltpu.VMEM((NH, NY - 1, rows, width), BF16)] * 2
        + [pltpu.VMEM((6, half, width), BF16)] * 2
        + [pltpu.VMEM((2, half, width), F32)]
        + [dma((NH, NY - 1))] * 2
        + [dma((6,))] * 2
    )


def gradient_scratch(size):
    dma = pltpu.SemaphoreType.DMA
    members, lanes = NX * NY * NC, 128
    chunk = (size // members // lanes, lanes)
    return [
        pltpu.VMEM((count,) + chunk if count else chunk, F32)
        for count in (members, members - 1, 0, NEAR, 0, NZ * NH // NEAR, 0, members)
    ] + [dma((4,))] * 2


def whole_kernel(f_ref, adj_ref, coords_ref, counts_ref, w_ref, cot_ref, act_ref, grad_ref, *scratch):
    adj_v, coords_v, coords_s, counts_s, plan_v, plan_s, w_v, cot_v, sums, in_sem, told, feat_v, *rest = scratch
    gather_sems, rest = rest[:10], rest[10:]
    reduce_refs, gradient_refs = rest[:9], rest[9:]
    p = Place()
    slots = adj_v.shape[0]
    pairs = (
        (coords_ref, coords_v), (coords_ref, coords_s), (counts_ref, counts_s), (f_ref, feat_v.at[pl.ds(2 * p.r, 2)]),
        (adj_ref, adj_v), (w_ref, w_v), (cot_ref, cot_v),
    )
    fetches = [pltpu.make_async_copy(a, b, in_sem.at[i]) for i, (a, b) in enumerate(pairs)]
    meet(p)
    gather = Gather(p, f_ref, feat_v, *gather_sems)
    gather.begin()
    tell(p, told.at[0], NEAR)
    for fetch in fetches:
        fetch.start()
    gather.go_on(0, 2)
    hear(p, told.at[0], NEAR)
    tell(p, told.at[1], 2 * NEAR)
    sums[slots] = jnp.zeros(sums.shape[1:], F32)
    for fetch in fetches[:3]:
        fetch.wait()
    find_links(coords_v[...], counts_s[p.c, p.r], plan_v)
    links = pltpu.make_async_copy(plan_v, plan_s, in_sem.at[0])
    links.start()
    gather.go_on(2, NZ)
    links.wait()
    hear(p, told.at[1], 2 * NEAR)
    for fetch in fetches[3:]:
        fetch.wait()
    gather.finish()
    multiply(coords_s, plan_s, adj_v, feat_v, sums)
    total, reduce_drain = reduce_rows(p, plan_s, sums, *reduce_refs)
    rounded = jnp.concatenate([total(0).astype(BF16), total(1).astype(BF16)], axis=0)
    apply_layer(rounded, w_v[...], cot_v[...], act_ref, gradient_refs[0])

    def drain():
        gather.drain()
        reduce_drain()

    sum_gradient(p, *gradient_refs, drain)
    write_gradient(gradient_refs[7], grad_ref)


def body(features, adj_blocks, block_coords, counts, weight, cotangent):
    tile_blocks, tile_coords = adj_blocks[0, 0], block_coords[0, 0]
    slots, block, _ = tile_blocks.shape
    rows, width = features.shape
    dma = pltpu.SemaphoreType.DMA
    vmem, hbm = pl.BlockSpec(memory_space=pltpu.VMEM), pl.BlockSpec(memory_space=pl.ANY)
    return pl.pallas_call(
        whole_kernel,
        out_shape=(
            jax.ShapeDtypeStruct(cotangent.shape, BF16),
            jax.ShapeDtypeStruct(weight.shape, F32),
        ),
        in_specs=[hbm] * 6,
        out_specs=(vmem, vmem),
        scratch_shapes=[
            pltpu.VMEM(tile_blocks.shape, BF16),
            pltpu.VMEM(tile_coords.shape, jnp.int32),
            pltpu.SMEM(tile_coords.shape, jnp.int32),
            pltpu.SMEM(counts.shape[::-1], jnp.int32),
            pltpu.VMEM((2, 128), jnp.int32),
            pltpu.SMEM((2, 128), jnp.int32),
            pltpu.VMEM(weight.shape, BF16),
            pltpu.VMEM(cotangent.shape, BF16),
            pltpu.VMEM((slots + 1, block, width), F32),
            dma((7,)),
            pltpu.SemaphoreType.REGULAR((2,)),
        ]
        + gather_scratch(rows, width)
        + reduce_scratch(rows, width)
        + gradient_scratch(weight.size),
        compiler_params=pltpu.CompilerParams(
            collective_id=0, has_side_effects=True, vmem_limit_bytes=60 << 20
        ),
        name="graph_convolution",
    )(features.reshape(2, rows // 2, width), tile_blocks, tile_coords, counts.T, weight, cotangent)


def solution(mesh):
    return jax.shard_map(
        body,
        mesh=mesh,
        in_specs=(
            P(("col", "row"), None),
            P("row", "col", None, None, None),
            P("row", "col", None, None),
            P(),
            P(),
            P(("row", "col"), None),
        ),
        out_specs=(P(("row", "col"), None), P()),
        check_vma=False,
    )
```

```python
import jax
import jax.numpy as jnp
from jax import lax
from jax.experimental import pallas as pl
from jax.experimental.pallas import tpu as pltpu
from jax.sharding import PartitionSpec as P

NX, NZ, NC = 4, 8, 2
NY, NH = 4, 4
NEAR = 4
PAIR = 2
UNROLL = 8
MESH = pl.DeviceIdType.MESH
F32, BF16 = jnp.float32, jnp.bfloat16


def remote(src, dst, send_sem, recv_sem, device):
    return pltpu.make_async_remote_copy(
        src_ref=src, dst_ref=dst, send_sem=send_sem, recv_sem=recv_sem, device_id=device, device_id_type=MESH
    )


class Place:
    def __init__(self):
        self.r, self.c = lax.axis_index("row"), lax.axis_index("col")
        self.x, self.z, self.core = self.r // (NZ * NC), (self.r // NC) % NZ, self.r % NC
        self.y, self.h = self.c // NH, self.c % NH
        self.members = NX * NY * NC
        self.me = (self.x * NY + self.y) * NC + self.core
        self.tall = NZ * NH
        self.level = self.h * NZ + self.z
        self.near, self.team = self.level % NEAR, self.level // NEAR

    def slot(self, x, z, core=None):
        return ((x % NX) * NZ + z) * NC + (self.core if core is None else core)

    def shelf(self, x, z, core=None):
        return ((self.core if core is None else core) * NX + x % NX) * NZ + z

    def in_column(self, x, z, core=None):
        return {"row": self.slot(x, z, core), "col": self.c}

    def member(self, m):
        return {
            "row": ((m // (NY * NC)) * NZ + self.z) * NC + m % NC,
            "col": ((m // NC) % NY) * NH + self.h,
        }

    def at_level(self, t):
        return {"row": (self.x * NZ + t % NZ) * NC + self.core, "col": self.y * NH + t // NZ}

    def up(self, steps):
        return self.at_level((self.level + steps) % self.tall)

    def at_y(self, y):
        return {"row": self.r, "col": (y % NY) * NH + self.h}

    def at_h(self, h):
        return {"row": self.r, "col": self.y * NH + h % NH}

    def offsets(self, steps):
        return sorted({s % self.tall for s in steps} - {0})


def neighbours(p, steps):
    return [p.at_y(p.y + 1), p.at_y(p.y + NY - 1)] + [p.up(s) for s in p.offsets(steps)]


def meet(p):
    barrier = pltpu.get_barrier_semaphore()
    devices = neighbours(p, (-NEAR, -1, 1, NEAR)) + [
        p.in_column(p.x, p.z, 1 - p.core), p.in_column(p.x + 1, p.z), p.in_column(p.x - 1, p.z)
    ]
    for device in devices:
        pl.semaphore_signal(barrier, inc=1, device_id=device, device_id_type=MESH)
    pl.semaphore_wait(barrier, len(devices))


def tell(p, sem):
    for device in neighbours(p, (-NEAR, NEAR)):
        pl.semaphore_signal(sem, inc=1, device_id=device, device_id_type=MESH)


def hear(p, sem):
    pl.semaphore_wait(sem, len(neighbours(p, (-NEAR, NEAR))))


class Gather:
    def __init__(self, p, f_ref, out_ref, zu_s, zu_r, zd_s, zd_r, xs_s, xs_r, xf_s, xf_r, cc_s, cc_r):
        self.p, self.f_ref, self.out_ref = p, f_ref, out_ref
        self.zu_s, self.zu_r, self.zd_s, self.zd_r = zu_s, zu_r, zd_s, zd_r
        self.xs_s, self.xs_r, self.xf_s, self.xf_r, self.cc_s, self.cc_r = xs_s, xs_r, xf_s, xf_r, cc_s, cc_r
        self.has_up, self.has_down = p.z < NZ - 1, p.z > 0
        self.far_up, self.far_down = p.z + NEAR < NZ, p.z - NEAR >= 0
        self.right, self.left = p.in_column(p.x + 1, p.z), p.in_column(p.x - 1, p.z)
        self.other = p.in_column(p.x, p.z, 1 - p.core)

    def send(self, s, b, send_sem, recv_sem, device, own=False):
        there = self.out_ref.at[2 * s + b]
        return remote(self.f_ref.at[b] if own else there, there, send_sem, recv_sem, device)

    def shards(self, s, count=1):
        return self.out_ref.at[pl.ds(2 * s, 2 * count)]

    def z_up(self, d, b, own=False, steps=1):
        k = d + steps - 1
        device = self.p.in_column(self.p.x, self.p.z + steps)
        return self.send(self.p.shelf(self.p.x, self.p.z - d), b, self.zu_s.at[k, b], self.zu_r.at[k, b], device, own)

    def z_down(self, d, b, own=False, steps=1):
        k = d + steps - 1
        device = self.p.in_column(self.p.x, self.p.z - steps)
        return self.send(self.p.shelf(self.p.x, self.p.z + d), b, self.zd_s.at[k, b], self.zd_r.at[k, b], device, own)

    def z_up_arrival(self, d, b):
        s = self.p.shelf(self.p.x, self.p.z - d)
        return self.send(s, b, self.zu_s.at[d - 1, b], self.zu_r.at[d - 1, b], self.other)

    def z_down_arrival(self, d, b):
        s = self.p.shelf(self.p.x, self.p.z + d)
        return self.send(s, b, self.zd_s.at[d - 1, b], self.zd_r.at[d - 1, b], self.other)

    def x_copy(self, z, way, own=False):
        device = self.right if way == 0 else self.left
        there = self.shards(self.p.shelf(self.p.x, z))
        return remote(self.f_ref if own else there, there, self.xs_s.at[way, z], self.xs_r.at[way, z], device)

    def x_arrival(self, z, way):
        here = self.shards(self.p.shelf(self.p.x - 1 if way == 0 else self.p.x + 1, z))
        return remote(here, here, self.xs_s.at[way, z], self.xs_r.at[way, z], self.right)

    def x_forward(self, z, way):
        s = self.p.shelf(self.p.x - 1 if way == 0 else self.p.x + 1, z)
        device = self.right if way == 0 else self.left
        return self.send(s, way, self.xf_s.at[way, z], self.xf_r.at[way, z], device)

    def f_arrival(self, z, way):
        return self.send(self.p.shelf(self.p.x + 2, z), way, self.xf_s.at[way, z], self.xf_r.at[way, z], self.right)

    def cross(self, dx, q, theirs=False):
        count = PAIR if dx == 2 else NZ // 2
        core = 1 - self.p.core if theirs else self.p.core
        there = self.shards(self.p.shelf(self.p.x + dx, q * count, core), count)
        return remote(there, there, self.cc_s.at[dx, q], self.cc_r.at[dx, q], self.other)

    def begin(self):
        for b in range(2):
            pl.when(self.has_up)(lambda b=b: self.z_up(0, b, True).start())
            pl.when(self.has_down)(lambda b=b: self.z_down(0, b, True).start())
        for way in range(2):
            self.x_copy(self.p.z, way, True).start()
        for b in range(2):
            pl.when(self.far_up)(lambda b=b: self.z_up(0, b, True, NEAR).start())
            pl.when(self.far_down)(lambda b=b: self.z_down(0, b, True, NEAR).start())

    def along_z(self, d, use):
        z = self.p.z
        below, above = jnp.logical_and(use, z - d >= 0), jnp.logical_and(use, z + d < NZ)
        on = d != NEAR - 1
        for b in range(2):

            @pl.when(below)
            def _():
                self.z_up_arrival(d, b).wait_recv()
                pl.when(jnp.logical_and(on, self.has_up))(lambda: self.z_up(d, b).start())
                if b == 1:
                    self.x_copy(z - d, 0).start()
                    self.x_copy(z - d, 1).start()

            @pl.when(above)
            def _():
                self.z_down_arrival(d, b).wait_recv()
                pl.when(jnp.logical_and(on, self.has_down))(lambda: self.z_down(d, b).start())
                if b == 1:
                    self.x_copy(z + d, 0).start()
                    self.x_copy(z + d, 1).start()

    def along_x(self, z):
        for way in range(2):
            self.x_arrival(z, way).wait_recv()
            self.x_forward(z, way).start()

    def last_halves(self, q):
        for i in range(PAIR):
            for way in range(2):
                self.f_arrival(q * PAIR + i, way).wait_recv()
        self.cross(2, q).start()

    def at_distance(self, d, act, use=True, at=None, end=None):
        at, end = (self.p.z, NZ) if at is None else (at, end)
        pl.when(jnp.logical_and(use, at - d >= 0))(lambda: act(at - d))
        pl.when(jnp.logical_and(use, jnp.logical_and(d > 0, at + d < end)))(lambda: act(at + d))

    def go_on(self, first, end):
        def distance(k):
            return k // 2 + 1 + (NEAR - 1) * (k % 2)

        def step(k, carry):
            self.along_z(distance(k), k != NZ - 2)
            pl.when(k == 1)(lambda: self.along_x(self.p.z))
            self.at_distance(distance(k - 2), self.along_x, k >= 2)
            return carry

        lax.fori_loop(first, end, step, 0)

    def cross_columns(self, act):
        for dx in (0, 1, NX - 1):
            for q in range(2):
                act(dx, q)

    def finish(self, own):
        own.wait()
        for q in range(2):
            self.cross(0, q).start()
        self.at_distance(NZ - 1, self.along_x)
        for dx in (1, NX - 1):
            for q in range(2):
                self.cross(dx, q).start()

        def last(d, carry):
            self.at_distance(d, self.last_halves, True, self.p.z // PAIR, NZ // PAIR)
            return carry

        lax.fori_loop(0, NZ // PAIR, last, 0)
        self.cross_columns(lambda dx, q: self.cross(dx, q, True).wait_recv())
        for q in range(NZ // PAIR):
            self.cross(2, q, True).wait_recv()

    def drain(self):
        z = self.p.z
        self.cross_columns(lambda dx, q: self.cross(dx, q).wait_send())
        for q in range(NZ // PAIR):
            self.cross(2, q).wait_send()

        def sent(k, carry):
            for way in range(2):
                self.x_forward(k, way).wait_send()
                self.x_copy(k, way).wait_send()
            on = jnp.logical_and(k != NEAR - 1, jnp.logical_and(self.has_up, k <= z))
            back = jnp.logical_and(k != NEAR - 1, jnp.logical_and(self.has_down, k <= NZ - 1 - z))
            for b in range(2):
                pl.when(on)(lambda b=b: self.z_up(k, b).wait_send())
                pl.when(back)(lambda b=b: self.z_down(k, b).wait_send())
            return carry

        lax.fori_loop(0, NZ, sent, 0)
        for b in range(2):
            pl.when(self.far_up)(lambda b=b: self.z_up(0, b, True, NEAR).wait_send())
            pl.when(self.far_down)(lambda b=b: self.z_down(0, b, True, NEAR).wait_send())


def find_links(coords, live, plan_ref):
    slots, wide = coords.shape[1], plan_ref.shape[1]
    rows = jnp.broadcast_to(coords[0:1, :], (slots, slots))
    down = lax.broadcasted_iota(jnp.int32, (slots, slots), 0)
    across = lax.broadcasted_iota(jnp.int32, (slots, slots), 1)
    row_of = jnp.sum(jnp.where(down == across, rows, 0), axis=1, keepdims=True)
    earlier = jnp.logical_and(row_of == rows, down < across)
    before = jnp.max(jnp.where(earlier, down, -1), axis=0, keepdims=True)
    plan_ref[...] = jnp.full(plan_ref.shape, slots, jnp.int32)
    plan_ref[0:1, 0:slots] = jnp.where(before < 0, slots, before)
    cols = coords[1:2, :]
    core = (cols // 2) % NC
    plan_ref[0:1, slots : 2 * slots] = (core * NX * NZ + cols // (2 * NC)) * 2 + cols % 2
    place = lax.broadcasted_iota(jnp.int32, (slots, wide), 1)
    slot = lax.broadcasted_iota(jnp.int32, (slots, wide), 0)
    named = jnp.logical_and(row_of == place, slot < live)
    last = jnp.max(jnp.where(named, slot, -1), axis=0, keepdims=True)
    plan_ref[1:2, :] = jnp.where(last < 0, slots, last)


def multiply(plan, adj_v, feat_v, sums):
    def turn(g, carry):
        first = g * UNROLL
        products = [
            jnp.dot(adj_v[first + i], feat_v[plan[0, adj_v.shape[0] + first + i]], preferred_element_type=F32)
            for i in range(UNROLL)
        ]
        for i in range(UNROLL):
            sums[first + i] = products[i] + sums[plan[0, first + i]]
        return carry

    lax.fori_loop(0, adj_v.shape[0] // UNROLL, turn, 0)


def reduce_rows(p, plan, sums, ysend, yrecv, zsend, zrecv, own_ref, ys_s, ys_r, zs_s, zs_r):
    half = sums.shape[1]

    def part(dy, k, b):
        block_row = (((p.y + dy) % NY) * NH + (p.h + k) % NH) * 2 + b
        return sums[plan[1, block_row]]

    def y_copy(k, dy):
        i = dy - 1
        return remote(ysend.at[k, i], yrecv.at[k, i], ys_s.at[k, i], ys_r.at[k, i], p.at_y(p.y + dy))

    def y_start(k):
        for dy in (2, 1, 3):
            for b in range(2):
                ysend[k, dy - 1, pl.ds(b * half, half)] = part(dy, k, b).astype(BF16)
            y_copy(k, dy).start()

    def y_end(k):
        for dy in range(1, NY):
            y_copy(k, dy).wait_recv()

    def y_sum(k, b):
        total = part(0, k, b)
        for i in range(NY - 1):
            total = total + yrecv[k, i, pl.ds(b * half, half)].astype(F32)
        return total

    def z_copy(i):
        device = p.at_h(p.h + (1 if i % 2 == 0 else NH - 1))
        return remote(zsend.at[i], zrecv.at[i], zs_s.at[i], zs_r.at[i], device)

    def z_start(i, value):
        zsend[i] = value.astype(BF16)
        z_copy(i).start()

    y_start(2)
    y_start(1)
    y_end(2)
    z_start(0, y_sum(2, 0))
    z_start(1, y_sum(2, 1))
    y_start(3)
    y_start(0)
    y_end(1)
    z_start(2, y_sum(1, 1))
    y_end(3)
    z_start(3, y_sum(3, 0))
    own_ref[0] = y_sum(1, 0)
    own_ref[1] = y_sum(3, 1)
    z_copy(0).wait_recv()
    z_start(4, own_ref[0] + zrecv[0].astype(F32))
    z_copy(1).wait_recv()
    z_start(5, own_ref[1] + zrecv[1].astype(F32))
    y_end(0)
    own_ref[0] = y_sum(0, 0)
    own_ref[1] = y_sum(0, 1)

    def drain():
        for k in range(NH):
            for dy in range(1, NY):
                y_copy(k, dy).wait_send()
        for i in range(6):
            z_copy(i).wait_send()

    def total(b):
        first, second = ((3, 4), (2, 5))[b]
        z_copy(first).wait_recv()
        z_copy(second).wait_recv()
        return own_ref[b] + zrecv[first].astype(F32) + zrecv[second].astype(F32)

    return total, drain


def silu_slope(preact, sigmoid_value):
    return sigmoid_value * (1.0 + preact * (1.0 - sigmoid_value))


def apply_layer(rounded, weight, cotangent, act_ref, grad_v):
    preact = jnp.dot(rounded, weight, preferred_element_type=F32)
    sigmoid_value = 1.0 / (1.0 + jnp.exp(-preact))
    act_ref[...] = (preact * sigmoid_value).astype(BF16)
    slope_grad = (cotangent.astype(F32) * silu_slope(preact, sigmoid_value)).astype(BF16)
    local_grad = lax.dot_general(rounded, slope_grad, (((0,), (0,)), ((), ())), preferred_element_type=F32)
    members, chunk, lanes = grad_v.shape
    per = members * lanes // local_grad.shape[1]
    for i in range(members // per):
        grad_v[i * per : (i + 1) * per] = local_grad[:, i * lanes : (i + 1) * lanes].reshape(per, chunk, lanes)


def sum_gradient(p, grad_v, r1, c1, r2, c2, r3, c3, r4, g_s, g_r, meanwhile):
    far = p.tall // NEAR

    def all_of(count, k):
        return remote(r1.at[:count], r1.at[:count], g_s.at[k], g_r.at[k], p.member(p.me))

    def scatter(j, carry):
        m = (p.me + j) % p.members
        remote(grad_v.at[m], r1.at[j - 1], g_s.at[0], g_r.at[0], p.member(m)).start()
        return carry

    lax.fori_loop(1, p.members, scatter, 0)
    all_of(p.members - 1, 0).wait_recv()
    c1[...] = grad_v[p.me] + jnp.sum(r1[...], axis=0)
    for j in range(1, NEAR):
        there = p.at_level(p.team * NEAR + (p.near + j) % NEAR)
        remote(c1, r2.at[p.near], g_s.at[1], g_r.at[1], there).start()
    r2[p.near] = c1[...]
    all_of(NEAR - 1, 1).wait_recv()
    c2[...] = jnp.sum(r2[...], axis=0)
    for j in sorted(range(1, far), key=lambda j: -min(j, far - j)):
        remote(c2, r3.at[p.team], g_s.at[2], g_r.at[2], p.up(j * NEAR)).start()
    r3[p.team] = c2[...]
    meanwhile()
    all_of(p.members - 1, 0).wait_send()
    all_of(NEAR - 1, 1).wait_send()
    all_of(far - 1, 2).wait_recv()
    c3[...] = jnp.sum(r3[...], axis=0)

    def hand_out(j, carry):
        remote(c3, r4.at[p.me], g_s.at[3], g_r.at[3], p.member((p.me + j) % p.members)).start()
        return carry

    lax.fori_loop(1, p.members, hand_out, 0)
    r4[p.me] = c3[...]
    all_of(far - 1, 2).wait_send()
    all_of(p.members - 1, 3).wait_recv()
    all_of(p.members - 1, 3).wait_send()


def write_gradient(r4, grad_ref):
    members, chunk, lanes = r4.shape
    per = grad_ref.shape[0] // chunk
    for i in range(members // per):
        grad_ref[:, i * lanes : (i + 1) * lanes] = r4[i * per : (i + 1) * per].reshape(per * chunk, lanes)


def gather_scratch(rows, width):
    dma = pltpu.SemaphoreType.DMA
    return (
        [pltpu.VMEM((2 * NX * NZ * NC, rows // 2, width), BF16)]
        + [dma((NZ, 2))] * 4
        + [dma((2, NZ))] * 4
        + [dma((NX, NZ // PAIR))] * 2
    )


def reduce_scratch(rows, width):
    dma = pltpu.SemaphoreType.DMA
    half = rows // 2
    return (
        [pltpu.VMEM((NH, NY - 1, rows, width), BF16)] * 2
        + [pltpu.VMEM((6, half, width), BF16)] * 2
        + [pltpu.VMEM((2, half, width), F32)]
        + [dma((NH, NY - 1))] * 2
        + [dma((6,))] * 2
    )


def gradient_scratch(size):
    dma = pltpu.SemaphoreType.DMA
    members, lanes = NX * NY * NC, 128
    chunk = (size // members // lanes, lanes)
    return [
        pltpu.VMEM((count,) + chunk if count else chunk, F32)
        for count in (members, members - 1, 0, NEAR, 0, NZ * NH // NEAR, 0, members)
    ] + [dma((4,))] * 2


def whole_kernel(f_ref, adj_ref, coords_ref, counts_ref, w_ref, cot_ref, act_ref, grad_ref, *scratch):
    adj_v, coords_v, counts_s, plan_v, plan_s, w_v, cot_v, sums, in_sem, told, feat_v, *rest = scratch
    gather_sems, rest = rest[:10], rest[10:]
    reduce_refs, gradient_refs = rest[:9], rest[9:]
    p = Place()
    slots = adj_v.shape[0]
    pairs = (
        (coords_ref, coords_v), (counts_ref, counts_s),
        (f_ref, feat_v.at[pl.ds(2 * p.shelf(p.x, p.z), 2)]),
        (adj_ref, adj_v), (w_ref, w_v), (cot_ref, cot_v),
    )
    fetches = [pltpu.make_async_copy(a, b, in_sem.at[i]) for i, (a, b) in enumerate(pairs)]
    meet(p)
    gather = Gather(p, f_ref, feat_v, *gather_sems)
    gather.begin()
    tell(p, told)
    for fetch in fetches:
        fetch.start()
    gather.go_on(0, 2)
    sums[slots] = jnp.zeros(sums.shape[1:], F32)
    for fetch in fetches[:2]:
        fetch.wait()
    find_links(coords_v[...], counts_s[p.c, p.r], plan_v)
    links = pltpu.make_async_copy(plan_v, plan_s, in_sem.at[0])
    links.start()
    gather.go_on(2, NZ)
    links.wait()
    hear(p, told)
    for fetch in fetches[3:]:
        fetch.wait()
    gather.finish(fetches[2])
    multiply(plan_s, adj_v, feat_v, sums)
    total, reduce_drain = reduce_rows(p, plan_s, sums, *reduce_refs)
    rounded = jnp.concatenate([total(0).astype(BF16), total(1).astype(BF16)], axis=0)
    apply_layer(rounded, w_v[...], cot_v[...], act_ref, gradient_refs[0])

    def drain():
        gather.drain()
        reduce_drain()

    sum_gradient(p, *gradient_refs, drain)
    write_gradient(gradient_refs[7], grad_ref)


def body(features, adj_blocks, block_coords, counts, weight, cotangent):
    tile_blocks, tile_coords = adj_blocks[0, 0], block_coords[0, 0]
    slots, block, _ = tile_blocks.shape
    rows, width = features.shape
    dma = pltpu.SemaphoreType.DMA
    vmem, hbm = pl.BlockSpec(memory_space=pltpu.VMEM), pl.BlockSpec(memory_space=pl.ANY)
    return pl.pallas_call(
        whole_kernel,
        out_shape=(
            jax.ShapeDtypeStruct(cotangent.shape, BF16),
            jax.ShapeDtypeStruct(weight.shape, F32),
        ),
        in_specs=[hbm] * 6,
        out_specs=(vmem, vmem),
        scratch_shapes=[
            pltpu.VMEM(tile_blocks.shape, BF16),
            pltpu.VMEM(tile_coords.shape, jnp.int32),
            pltpu.SMEM(counts.shape[::-1], jnp.int32),
            pltpu.VMEM((2, 128), jnp.int32),
            pltpu.SMEM((2, 128), jnp.int32),
            pltpu.VMEM(weight.shape, BF16),
            pltpu.VMEM(cotangent.shape, BF16),
            pltpu.VMEM((slots + 1, block, width), F32),
            dma((6,)),
            pltpu.SemaphoreType.REGULAR,
        ]
        + gather_scratch(rows, width)
        + reduce_scratch(rows, width)
        + gradient_scratch(weight.size),
        compiler_params=pltpu.CompilerParams(
            collective_id=0, has_side_effects=True, vmem_limit_bytes=60 << 20
        ),
        name="graph_convolution",
    )(features.reshape(2, rows // 2, width), tile_blocks, tile_coords, counts.T, weight, cotangent)


def solution(mesh):
    return jax.shard_map(
        body,
        mesh=mesh,
        in_specs=(
            P(("col", "row"), None),
            P("row", "col", None, None, None),
            P("row", "col", None, None),
            P(),
            P(),
            P(("row", "col"), None),
        ),
        out_specs=(P(("row", "col"), None), P()),
        check_vma=False,
    )
```

```python
import jax
import jax.numpy as jnp
from jax import lax
from jax.experimental import pallas as pl
from jax.experimental.pallas import tpu as pltpu
from jax.sharding import PartitionSpec as P

NX, NZ, NC = 4, 8, 2
NY, NH = 4, 4
NEAR = 4
PAIR = 2
UNROLL = 8
MESH = pl.DeviceIdType.MESH
F32, BF16 = jnp.float32, jnp.bfloat16


def remote(src, dst, send_sem, recv_sem, device):
    return pltpu.make_async_remote_copy(
        src_ref=src, dst_ref=dst, send_sem=send_sem, recv_sem=recv_sem, device_id=device, device_id_type=MESH
    )


class Place:
    def __init__(self):
        self.r, self.c = lax.axis_index("row"), lax.axis_index("col")
        self.x, self.z, self.core = self.r // (NZ * NC), (self.r // NC) % NZ, self.r % NC
        self.y, self.h = self.c // NH, self.c % NH
        self.members = NX * NY * NC
        self.me = (self.x * NY + self.y) * NC + self.core
        self.tall = NZ * NH
        self.level = self.h * NZ + self.z
        self.near, self.team = self.level % NEAR, self.level // NEAR

    def slot(self, x, z, core=None):
        return ((x % NX) * NZ + z) * NC + (self.core if core is None else core)

    def shelf(self, x, z, core=None):
        return ((self.core if core is None else core) * NX + x % NX) * NZ + z

    def in_column(self, x, z, core=None):
        return {"row": self.slot(x, z, core), "col": self.c}

    def member(self, m):
        return {
            "row": ((m // (NY * NC)) * NZ + self.z) * NC + m % NC,
            "col": ((m // NC) % NY) * NH + self.h,
        }

    def at_level(self, t):
        return {"row": (self.x * NZ + t % NZ) * NC + self.core, "col": self.y * NH + t // NZ}

    def up(self, steps):
        return self.at_level((self.level + steps) % self.tall)

    def at_y(self, y):
        return {"row": self.r, "col": (y % NY) * NH + self.h}

    def at_h(self, h):
        return {"row": self.r, "col": self.y * NH + h % NH}

    def offsets(self, steps):
        return sorted({s % self.tall for s in steps} - {0})


def neighbours(p, steps):
    return [p.at_y(p.y + 1), p.at_y(p.y + NY - 1)] + [p.up(s) for s in p.offsets(steps)]


def meet(p):
    barrier = pltpu.get_barrier_semaphore()
    devices = neighbours(p, (-NEAR, -1, 1, NEAR)) + [
        p.in_column(p.x, p.z, 1 - p.core), p.in_column(p.x + 1, p.z), p.in_column(p.x - 1, p.z)
    ]
    for device in devices:
        pl.semaphore_signal(barrier, inc=1, device_id=device, device_id_type=MESH)
    pl.semaphore_wait(barrier, len(devices))


def tell(p, sem):
    for device in neighbours(p, (-NEAR, NEAR)):
        pl.semaphore_signal(sem, inc=1, device_id=device, device_id_type=MESH)


def hear(p, sem):
    pl.semaphore_wait(sem, len(neighbours(p, (-NEAR, NEAR))))


class Gather:
    def __init__(self, p, f_ref, out_ref, zu_s, zu_r, zd_s, zd_r, xs_s, xs_r, xf_s, xf_r, cc_s, cc_r):
        self.p, self.f_ref, self.out_ref = p, f_ref, out_ref
        self.zu_s, self.zu_r, self.zd_s, self.zd_r = zu_s, zu_r, zd_s, zd_r
        self.xs_s, self.xs_r, self.xf_s, self.xf_r, self.cc_s, self.cc_r = xs_s, xs_r, xf_s, xf_r, cc_s, cc_r
        self.has_up, self.has_down = p.z < NZ - 1, p.z > 0
        self.far_up, self.far_down = p.z + NEAR < NZ, p.z - NEAR >= 0
        self.right, self.left = p.in_column(p.x + 1, p.z), p.in_column(p.x - 1, p.z)
        self.other = p.in_column(p.x, p.z, 1 - p.core)

    def send(self, s, b, send_sem, recv_sem, device, own=False):
        there = self.out_ref.at[2 * s + b]
        return remote(self.f_ref.at[b] if own else there, there, send_sem, recv_sem, device)

    def shards(self, s, count=1):
        return self.out_ref.at[pl.ds(2 * s, 2 * count)]

    def z_up(self, d, b, own=False, steps=1):
        k = d + steps - 1
        device = self.p.in_column(self.p.x, self.p.z + steps)
        return self.send(self.p.shelf(self.p.x, self.p.z - d), b, self.zu_s.at[k, b], self.zu_r.at[k, b], device, own)

    def z_down(self, d, b, own=False, steps=1):
        k = d + steps - 1
        device = self.p.in_column(self.p.x, self.p.z - steps)
        return self.send(self.p.shelf(self.p.x, self.p.z + d), b, self.zd_s.at[k, b], self.zd_r.at[k, b], device, own)

    def z_up_arrival(self, d, b):
        s = self.p.shelf(self.p.x, self.p.z - d)
        return self.send(s, b, self.zu_s.at[d - 1, b], self.zu_r.at[d - 1, b], self.other)

    def z_down_arrival(self, d, b):
        s = self.p.shelf(self.p.x, self.p.z + d)
        return self.send(s, b, self.zd_s.at[d - 1, b], self.zd_r.at[d - 1, b], self.other)

    def x_copy(self, z, way, own=False):
        device = self.right if way == 0 else self.left
        there = self.shards(self.p.shelf(self.p.x, z))
        return remote(self.f_ref if own else there, there, self.xs_s.at[way, z], self.xs_r.at[way, z], device)

    def x_arrival(self, z, way):
        here = self.shards(self.p.shelf(self.p.x - 1 if way == 0 else self.p.x + 1, z))
        return remote(here, here, self.xs_s.at[way, z], self.xs_r.at[way, z], self.right)

    def x_forward(self, z, way):
        s = self.p.shelf(self.p.x - 1 if way == 0 else self.p.x + 1, z)
        device = self.right if way == 0 else self.left
        return self.send(s, way, self.xf_s.at[way, z], self.xf_r.at[way, z], device)

    def f_arrival(self, z, way):
        return self.send(self.p.shelf(self.p.x + 2, z), way, self.xf_s.at[way, z], self.xf_r.at[way, z], self.right)

    def cross(self, dx, q, theirs=False):
        count = NZ // 2 if dx == 0 else PAIR
        core = 1 - self.p.core if theirs else self.p.core
        there = self.shards(self.p.shelf(self.p.x + dx, q * count, core), count)
        return remote(there, there, self.cc_s.at[dx, q], self.cc_r.at[dx, q], self.other)

    def begin(self):
        for b in range(2):
            pl.when(self.has_up)(lambda b=b: self.z_up(0, b, True).start())
            pl.when(self.has_down)(lambda b=b: self.z_down(0, b, True).start())
        for way in range(2):
            self.x_copy(self.p.z, way, True).start()
        for b in range(2):
            pl.when(self.far_up)(lambda b=b: self.z_up(0, b, True, NEAR).start())
            pl.when(self.far_down)(lambda b=b: self.z_down(0, b, True, NEAR).start())

    def along_z(self, d, use):
        z = self.p.z
        below, above = jnp.logical_and(use, z - d >= 0), jnp.logical_and(use, z + d < NZ)
        on = d != NEAR - 1
        for b in range(2):

            @pl.when(below)
            def _():
                self.z_up_arrival(d, b).wait_recv()
                pl.when(jnp.logical_and(on, self.has_up))(lambda: self.z_up(d, b).start())
                if b == 1:
                    self.x_copy(z - d, 0).start()
                    self.x_copy(z - d, 1).start()

            @pl.when(above)
            def _():
                self.z_down_arrival(d, b).wait_recv()
                pl.when(jnp.logical_and(on, self.has_down))(lambda: self.z_down(d, b).start())
                if b == 1:
                    self.x_copy(z + d, 0).start()
                    self.x_copy(z + d, 1).start()

    def along_x(self, q):
        for i in range(PAIR):
            for way in range(2):
                self.x_arrival(q * PAIR + i, way).wait_recv()
                self.x_forward(q * PAIR + i, way).start()
        self.cross(NX - 1, q).start()
        self.cross(1, q).start()

    def last_halves(self, q):
        for i in range(PAIR):
            for way in range(2):
                self.f_arrival(q * PAIR + i, way).wait_recv()
        self.cross(2, q).start()

    def pairs(self, act):
        at, end = self.p.z // PAIR, NZ // PAIR

        def step(d, carry):
            pl.when(at - d >= 0)(lambda: act(at - d))
            pl.when(jnp.logical_and(d > 0, at + d < end))(lambda: act(at + d))
            return carry

        lax.fori_loop(0, end, step, 0)

    def go_on(self, first, end):
        def distance(k):
            return k // 2 + 1 + (NEAR - 1) * (k % 2)

        def step(k, carry):
            self.along_z(distance(k), k != NZ - 2)
            return carry

        lax.fori_loop(first, end, step, 0)

    def crossings(self, act):
        for dx in range(NX):
            for q in range(2 if dx == 0 else NZ // PAIR):
                act(dx, q)

    def finish(self, own):
        own.wait()
        for q in range(2):
            self.cross(0, q).start()
        self.pairs(self.along_x)
        self.pairs(self.last_halves)
        self.crossings(lambda dx, q: self.cross(dx, q, True).wait_recv())

    def drain(self):
        z = self.p.z
        self.crossings(lambda dx, q: self.cross(dx, q).wait_send())

        def sent(k, carry):
            for way in range(2):
                self.x_forward(k, way).wait_send()
                self.x_copy(k, way).wait_send()
            on = jnp.logical_and(k != NEAR - 1, jnp.logical_and(self.has_up, k <= z))
            back = jnp.logical_and(k != NEAR - 1, jnp.logical_and(self.has_down, k <= NZ - 1 - z))
            for b in range(2):
                pl.when(on)(lambda b=b: self.z_up(k, b).wait_send())
                pl.when(back)(lambda b=b: self.z_down(k, b).wait_send())
            return carry

        lax.fori_loop(0, NZ, sent, 0)
        for b in range(2):
            pl.when(self.far_up)(lambda b=b: self.z_up(0, b, True, NEAR).wait_send())
            pl.when(self.far_down)(lambda b=b: self.z_down(0, b, True, NEAR).wait_send())


def find_links(coords, live, plan_ref):
    slots, wide = coords.shape[1], plan_ref.shape[1]
    rows = jnp.broadcast_to(coords[0:1, :], (slots, slots))
    down = lax.broadcasted_iota(jnp.int32, (slots, slots), 0)
    across = lax.broadcasted_iota(jnp.int32, (slots, slots), 1)
    row_of = jnp.sum(jnp.where(down == across, rows, 0), axis=1, keepdims=True)
    earlier = jnp.logical_and(row_of == rows, down < across)
    before = jnp.max(jnp.where(earlier, down, -1), axis=0, keepdims=True)
    plan_ref[...] = jnp.full(plan_ref.shape, slots, jnp.int32)
    plan_ref[0:1, 0:slots] = jnp.where(before < 0, slots, before)
    cols = coords[1:2, :]
    core = (cols // 2) % NC
    plan_ref[0:1, slots : 2 * slots] = (core * NX * NZ + cols // (2 * NC)) * 2 + cols % 2
    place = lax.broadcasted_iota(jnp.int32, (slots, wide), 1)
    slot = lax.broadcasted_iota(jnp.int32, (slots, wide), 0)
    named = jnp.logical_and(row_of == place, slot < live)
    last = jnp.max(jnp.where(named, slot, -1), axis=0, keepdims=True)
    plan_ref[1:2, :] = jnp.where(last < 0, slots, last)


def multiply(plan, adj_v, feat_v, sums):
    def turn(g, carry):
        first = g * UNROLL
        products = [
            jnp.dot(adj_v[first + i], feat_v[plan[0, adj_v.shape[0] + first + i]], preferred_element_type=F32)
            for i in range(UNROLL)
        ]
        for i in range(UNROLL):
            sums[first + i] = products[i] + sums[plan[0, first + i]]
        return carry

    lax.fori_loop(0, adj_v.shape[0] // UNROLL, turn, 0)


def reduce_rows(p, plan, sums, ysend, yrecv, zsend, zrecv, own_ref, ys_s, ys_r, zs_s, zs_r):
    half = sums.shape[1]

    def part(dy, k, b):
        block_row = (((p.y + dy) % NY) * NH + (p.h + k) % NH) * 2 + b
        return sums[plan[1, block_row]]

    def y_copy(k, dy):
        i = dy - 1
        return remote(ysend.at[k, i], yrecv.at[k, i], ys_s.at[k, i], ys_r.at[k, i], p.at_y(p.y + dy))

    def y_start(k):
        for dy in (2, 1, 3):
            for b in range(2):
                ysend[k, dy - 1, pl.ds(b * half, half)] = part(dy, k, b).astype(BF16)
            y_copy(k, dy).start()

    def y_end(k):
        for dy in range(1, NY):
            y_copy(k, dy).wait_recv()

    def y_sum(k, b):
        total = part(0, k, b)
        for i in range(NY - 1):
            total = total + yrecv[k, i, pl.ds(b * half, half)].astype(F32)
        return total

    def z_copy(i):
        device = p.at_h(p.h + (1 if i % 2 == 0 else NH - 1))
        return remote(zsend.at[i], zrecv.at[i], zs_s.at[i], zs_r.at[i], device)

    def z_start(i, value):
        zsend[i] = value.astype(BF16)
        z_copy(i).start()

    y_start(2)
    y_start(1)
    y_end(2)
    z_start(0, y_sum(2, 0))
    z_start(1, y_sum(2, 1))
    y_start(3)
    y_start(0)
    y_end(1)
    z_start(2, y_sum(1, 1))
    y_end(3)
    z_start(3, y_sum(3, 0))
    own_ref[0] = y_sum(1, 0)
    own_ref[1] = y_sum(3, 1)
    z_copy(0).wait_recv()
    z_start(4, own_ref[0] + zrecv[0].astype(F32))
    z_copy(1).wait_recv()
    z_start(5, own_ref[1] + zrecv[1].astype(F32))
    y_end(0)
    own_ref[0] = y_sum(0, 0)
    own_ref[1] = y_sum(0, 1)

    def drain():
        for k in range(NH):
            for dy in range(1, NY):
                y_copy(k, dy).wait_send()
        for i in range(6):
            z_copy(i).wait_send()

    def total(b):
        first, second = ((3, 4), (2, 5))[b]
        z_copy(first).wait_recv()
        z_copy(second).wait_recv()
        return own_ref[b] + zrecv[first].astype(F32) + zrecv[second].astype(F32)

    return total, drain


def silu_slope(preact, sigmoid_value):
    return sigmoid_value * (1.0 + preact * (1.0 - sigmoid_value))


def apply_layer(rounded, weight, cotangent, act_ref, grad_v):
    preact = jnp.dot(rounded, weight, preferred_element_type=F32)
    sigmoid_value = 1.0 / (1.0 + jnp.exp(-preact))
    act_ref[...] = (preact * sigmoid_value).astype(BF16)
    slope_grad = (cotangent.astype(F32) * silu_slope(preact, sigmoid_value)).astype(BF16)
    local_grad = lax.dot_general(rounded, slope_grad, (((0,), (0,)), ((), ())), preferred_element_type=F32)
    members, chunk, lanes = grad_v.shape
    per = members * lanes // local_grad.shape[1]
    for i in range(members // per):
        grad_v[i * per : (i + 1) * per] = local_grad[:, i * lanes : (i + 1) * lanes].reshape(per, chunk, lanes)


def sum_gradient(p, grad_v, r1, c1, r2, c2, r3, c3, r4, g_s, g_r, meanwhile):
    far = p.tall // NEAR

    def all_of(count, k):
        return remote(r1.at[:count], r1.at[:count], g_s.at[k], g_r.at[k], p.member(p.me))

    def scatter(j, carry):
        m = (p.me + j) % p.members
        remote(grad_v.at[m], r1.at[j - 1], g_s.at[0], g_r.at[0], p.member(m)).start()
        return carry

    lax.fori_loop(1, p.members, scatter, 0)
    all_of(p.members - 1, 0).wait_recv()
    c1[...] = grad_v[p.me] + jnp.sum(r1[...], axis=0)
    for j in range(1, NEAR):
        there = p.at_level(p.team * NEAR + (p.near + j) % NEAR)
        remote(c1, r2.at[p.near], g_s.at[1], g_r.at[1], there).start()
    r2[p.near] = c1[...]
    all_of(NEAR - 1, 1).wait_recv()
    c2[...] = jnp.sum(r2[...], axis=0)
    for j in sorted(range(1, far), key=lambda j: -min(j, far - j)):
        remote(c2, r3.at[p.team], g_s.at[2], g_r.at[2], p.up(j * NEAR)).start()
    r3[p.team] = c2[...]
    meanwhile()
    all_of(p.members - 1, 0).wait_send()
    all_of(NEAR - 1, 1).wait_send()
    all_of(far - 1, 2).wait_recv()
    c3[...] = jnp.sum(r3[...], axis=0)

    def hand_out(j, carry):
        remote(c3, r4.at[p.me], g_s.at[3], g_r.at[3], p.member((p.me + j) % p.members)).start()
        return carry

    lax.fori_loop(1, p.members, hand_out, 0)
    r4[p.me] = c3[...]
    all_of(far - 1, 2).wait_send()
    all_of(p.members - 1, 3).wait_recv()
    all_of(p.members - 1, 3).wait_send()


def write_gradient(r4, grad_ref):
    members, chunk, lanes = r4.shape
    per = grad_ref.shape[0] // chunk
    for i in range(members // per):
        grad_ref[:, i * lanes : (i + 1) * lanes] = r4[i * per : (i + 1) * per].reshape(per * chunk, lanes)


def gather_scratch(rows, width):
    dma = pltpu.SemaphoreType.DMA
    return (
        [pltpu.VMEM((2 * NX * NZ * NC, rows // 2, width), BF16)]
        + [dma((NZ, 2))] * 4
        + [dma((2, NZ))] * 4
        + [dma((NX, NZ // PAIR))] * 2
    )


def reduce_scratch(rows, width):
    dma = pltpu.SemaphoreType.DMA
    half = rows // 2
    return (
        [pltpu.VMEM((NH, NY - 1, rows, width), BF16)] * 2
        + [pltpu.VMEM((6, half, width), BF16)] * 2
        + [pltpu.VMEM((2, half, width), F32)]
        + [dma((NH, NY - 1))] * 2
        + [dma((6,))] * 2
    )


def gradient_scratch(size):
    dma = pltpu.SemaphoreType.DMA
    members, lanes = NX * NY * NC, 128
    chunk = (size // members // lanes, lanes)
    return [
        pltpu.VMEM((count,) + chunk if count else chunk, F32)
        for count in (members, members - 1, 0, NEAR, 0, NZ * NH // NEAR, 0, members)
    ] + [dma((4,))] * 2


def whole_kernel(f_ref, adj_ref, coords_ref, counts_ref, w_ref, cot_ref, act_ref, grad_ref, *scratch):
    adj_v, coords_v, counts_s, plan_v, plan_s, w_v, cot_v, sums, in_sem, told, feat_v, *rest = scratch
    gather_sems, rest = rest[:10], rest[10:]
    reduce_refs, gradient_refs = rest[:9], rest[9:]
    p = Place()
    slots = adj_v.shape[0]
    pairs = (
        (coords_ref, coords_v), (counts_ref, counts_s),
        (f_ref, feat_v.at[pl.ds(2 * p.shelf(p.x, p.z), 2)]),
        (adj_ref, adj_v), (w_ref, w_v), (cot_ref, cot_v),
    )
    fetches = [pltpu.make_async_copy(a, b, in_sem.at[i]) for i, (a, b) in enumerate(pairs)]
    meet(p)
    gather = Gather(p, f_ref, feat_v, *gather_sems)
    gather.begin()
    tell(p, told)
    for fetch in fetches:
        fetch.start()
    gather.go_on(0, 2)
    sums[slots] = jnp.zeros(sums.shape[1:], F32)
    for fetch in fetches[:2]:
        fetch.wait()
    find_links(coords_v[...], counts_s[p.c, p.r], plan_v)
    links = pltpu.make_async_copy(plan_v, plan_s, in_sem.at[0])
    links.start()
    gather.go_on(2, NZ)
    links.wait()
    hear(p, told)
    for fetch in fetches[3:]:
        fetch.wait()
    gather.finish(fetches[2])
    multiply(plan_s, adj_v, feat_v, sums)
    total, reduce_drain = reduce_rows(p, plan_s, sums, *reduce_refs)
    rounded = jnp.concatenate([total(0).astype(BF16), total(1).astype(BF16)], axis=0)
    apply_layer(rounded, w_v[...], cot_v[...], act_ref, gradient_refs[0])

    def drain():
        gather.drain()
        reduce_drain()

    sum_gradient(p, *gradient_refs, drain)
    write_gradient(gradient_refs[7], grad_ref)


def body(features, adj_blocks, block_coords, counts, weight, cotangent):
    tile_blocks, tile_coords = adj_blocks[0, 0], block_coords[0, 0]
    slots, block, _ = tile_blocks.shape
    rows, width = features.shape
    dma = pltpu.SemaphoreType.DMA
    vmem, hbm = pl.BlockSpec(memory_space=pltpu.VMEM), pl.BlockSpec(memory_space=pl.ANY)
    return pl.pallas_call(
        whole_kernel,
        out_shape=(
            jax.ShapeDtypeStruct(cotangent.shape, BF16),
            jax.ShapeDtypeStruct(weight.shape, F32),
        ),
        in_specs=[hbm] * 6,
        out_specs=(vmem, vmem),
        scratch_shapes=[
            pltpu.VMEM(tile_blocks.shape, BF16),
            pltpu.VMEM(tile_coords.shape, jnp.int32),
            pltpu.SMEM(counts.shape[::-1], jnp.int32),
            pltpu.VMEM((2, 128), jnp.int32),
            pltpu.SMEM((2, 128), jnp.int32),
            pltpu.VMEM(weight.shape, BF16),
            pltpu.VMEM(cotangent.shape, BF16),
            pltpu.VMEM((slots + 1, block, width), F32),
            dma((6,)),
            pltpu.SemaphoreType.REGULAR,
        ]
        + gather_scratch(rows, width)
        + reduce_scratch(rows, width)
        + gradient_scratch(weight.size),
        compiler_params=pltpu.CompilerParams(
            collective_id=0, has_side_effects=True, vmem_limit_bytes=60 << 20
        ),
        name="graph_convolution",
    )(features.reshape(2, rows // 2, width), tile_blocks, tile_coords, counts.T, weight, cotangent)


def solution(mesh):
    return jax.shard_map(
        body,
        mesh=mesh,
        in_specs=(
            P(("col", "row"), None),
            P("row", "col", None, None, None),
            P("row", "col", None, None),
            P(),
            P(),
            P(("row", "col"), None),
        ),
        out_specs=(P(("row", "col"), None), P()),
        check_vma=False,
    )
```

```python
import jax
import jax.numpy as jnp
from jax import lax
from jax.experimental import pallas as pl
from jax.experimental.pallas import tpu as pltpu
from jax.sharding import PartitionSpec as P

NX, NZ, NC = 4, 8, 2
NY, NH = 4, 4
NEAR = 4
PAIR = 2
UNROLL = 16
MESH = pl.DeviceIdType.MESH
F32, BF16 = jnp.float32, jnp.bfloat16


def remote(src, dst, send_sem, recv_sem, device):
    return pltpu.make_async_remote_copy(
        src_ref=src, dst_ref=dst, send_sem=send_sem, recv_sem=recv_sem, device_id=device, device_id_type=MESH
    )


class Place:
    def __init__(self):
        self.r, self.c = lax.axis_index("row"), lax.axis_index("col")
        self.x, self.z, self.core = self.r // (NZ * NC), (self.r // NC) % NZ, self.r % NC
        self.y, self.h = self.c // NH, self.c % NH
        self.members = NX * NY * NC
        self.me = (self.x * NY + self.y) * NC + self.core
        self.tall = NZ * NH
        self.level = self.h * NZ + self.z
        self.near, self.team = self.level % NEAR, self.level // NEAR

    def slot(self, x, z, core=None):
        return ((x % NX) * NZ + z) * NC + (self.core if core is None else core)

    def shelf(self, x, z, core=None):
        return ((self.core if core is None else core) * NX + x % NX) * NZ + z

    def in_column(self, x, z, core=None):
        return {"row": self.slot(x, z, core), "col": self.c}

    def member(self, m):
        return {
            "row": ((m // (NY * NC)) * NZ + self.z) * NC + m % NC,
            "col": ((m // NC) % NY) * NH + self.h,
        }

    def at_level(self, t):
        return {"row": (self.x * NZ + t % NZ) * NC + self.core, "col": self.y * NH + t // NZ}

    def up(self, steps):
        return self.at_level((self.level + steps) % self.tall)

    def at_y(self, y):
        return {"row": self.r, "col": (y % NY) * NH + self.h}

    def at_h(self, h):
        return {"row": self.r, "col": self.y * NH + h % NH}

    def offsets(self, steps):
        return sorted({s % self.tall for s in steps} - {0})


def neighbours(p, steps):
    return [p.at_y(p.y + 1), p.at_y(p.y + NY - 1)] + [p.up(s) for s in p.offsets(steps)]


def meet(p):
    barrier = pltpu.get_barrier_semaphore()
    devices = neighbours(p, (-NEAR, -1, 1, NEAR)) + [
        p.in_column(p.x, p.z, 1 - p.core), p.in_column(p.x + 1, p.z), p.in_column(p.x - 1, p.z)
    ]
    for device in devices:
        pl.semaphore_signal(barrier, inc=1, device_id=device, device_id_type=MESH)
    pl.semaphore_wait(barrier, len(devices))


def tell(p, sem):
    for device in neighbours(p, (-NEAR, NEAR)):
        pl.semaphore_signal(sem, inc=1, device_id=device, device_id_type=MESH)


def hear(p, sem):
    pl.semaphore_wait(sem, len(neighbours(p, (-NEAR, NEAR))))


class Gather:
    def __init__(self, p, f_ref, out_ref, zu_s, zu_r, zd_s, zd_r, xs_s, xs_r, xf_s, xf_r, cc_s, cc_r):
        self.p, self.f_ref, self.out_ref = p, f_ref, out_ref
        self.zu_s, self.zu_r, self.zd_s, self.zd_r = zu_s, zu_r, zd_s, zd_r
        self.xs_s, self.xs_r, self.xf_s, self.xf_r, self.cc_s, self.cc_r = xs_s, xs_r, xf_s, xf_r, cc_s, cc_r
        self.has_up, self.has_down = p.z < NZ - 1, p.z > 0
        self.far_up, self.far_down = p.z + NEAR < NZ, p.z - NEAR >= 0
        self.right, self.left = p.in_column(p.x + 1, p.z), p.in_column(p.x - 1, p.z)
        self.other = p.in_column(p.x, p.z, 1 - p.core)

    def send(self, s, b, send_sem, recv_sem, device, own=False):
        there = self.out_ref.at[2 * s + b]
        return remote(self.f_ref.at[b] if own else there, there, send_sem, recv_sem, device)

    def shards(self, s, count=1):
        return self.out_ref.at[pl.ds(2 * s, 2 * count)]

    def z_up(self, d, b, own=False, steps=1):
        k = d + steps - 1
        device = self.p.in_column(self.p.x, self.p.z + steps)
        return self.send(self.p.shelf(self.p.x, self.p.z - d), b, self.zu_s.at[k, b], self.zu_r.at[k, b], device, own)

    def z_down(self, d, b, own=False, steps=1):
        k = d + steps - 1
        device = self.p.in_column(self.p.x, self.p.z - steps)
        return self.send(self.p.shelf(self.p.x, self.p.z + d), b, self.zd_s.at[k, b], self.zd_r.at[k, b], device, own)

    def z_up_arrival(self, d, b):
        s = self.p.shelf(self.p.x, self.p.z - d)
        return self.send(s, b, self.zu_s.at[d - 1, b], self.zu_r.at[d - 1, b], self.other)

    def z_down_arrival(self, d, b):
        s = self.p.shelf(self.p.x, self.p.z + d)
        return self.send(s, b, self.zd_s.at[d - 1, b], self.zd_r.at[d - 1, b], self.other)

    def x_copy(self, z, way, own=False):
        device = self.right if way == 0 else self.left
        there = self.shards(self.p.shelf(self.p.x, z))
        return remote(self.f_ref if own else there, there, self.xs_s.at[way, z], self.xs_r.at[way, z], device)

    def x_arrival(self, z, way):
        here = self.shards(self.p.shelf(self.p.x - 1 if way == 0 else self.p.x + 1, z))
        return remote(here, here, self.xs_s.at[way, z], self.xs_r.at[way, z], self.right)

    def x_forward(self, z, way):
        s = self.p.shelf(self.p.x - 1 if way == 0 else self.p.x + 1, z)
        device = self.right if way == 0 else self.left
        return self.send(s, way, self.xf_s.at[way, z], self.xf_r.at[way, z], device)

    def f_arrival(self, z, way):
        return self.send(self.p.shelf(self.p.x + 2, z), way, self.xf_s.at[way, z], self.xf_r.at[way, z], self.right)

    def cross(self, dx, q, theirs=False):
        count = NZ // 2 if dx == 0 else PAIR
        core = 1 - self.p.core if theirs else self.p.core
        there = self.shards(self.p.shelf(self.p.x + dx, q * count, core), count)
        return remote(there, there, self.cc_s.at[dx, q], self.cc_r.at[dx, q], self.other)

    def begin(self):
        for b in range(2):
            pl.when(self.has_up)(lambda b=b: self.z_up(0, b, True).start())
            pl.when(self.has_down)(lambda b=b: self.z_down(0, b, True).start())
        for way in range(2):
            self.x_copy(self.p.z, way, True).start()
        for b in range(2):
            pl.when(self.far_up)(lambda b=b: self.z_up(0, b, True, NEAR).start())
            pl.when(self.far_down)(lambda b=b: self.z_down(0, b, True, NEAR).start())

    def along_z(self, d, use):
        z = self.p.z
        below, above = jnp.logical_and(use, z - d >= 0), jnp.logical_and(use, z + d < NZ)
        on = d != NEAR - 1
        for b in range(2):

            @pl.when(below)
            def _():
                self.z_up_arrival(d, b).wait_recv()
                pl.when(jnp.logical_and(on, self.has_up))(lambda: self.z_up(d, b).start())
                if b == 1:
                    self.x_copy(z - d, 0).start()
                    self.x_copy(z - d, 1).start()

            @pl.when(above)
            def _():
                self.z_down_arrival(d, b).wait_recv()
                pl.when(jnp.logical_and(on, self.has_down))(lambda: self.z_down(d, b).start())
                if b == 1:
                    self.x_copy(z + d, 0).start()
                    self.x_copy(z + d, 1).start()

    def along_x(self, q):
        for i in range(PAIR):
            for way in range(2):
                self.x_arrival(q * PAIR + i, way).wait_recv()
                self.x_forward(q * PAIR + i, way).start()
        self.cross(NX - 1, q).start()
        self.cross(1, q).start()

    def last_halves(self, q):
        for i in range(PAIR):
            for way in range(2):
                self.f_arrival(q * PAIR + i, way).wait_recv()
        self.cross(2, q).start()

    def pairs(self, act):
        at, end = self.p.z // PAIR, NZ // PAIR

        def step(d, carry):
            pl.when(at - d >= 0)(lambda: act(at - d))
            pl.when(jnp.logical_and(d > 0, at + d < end))(lambda: act(at + d))
            return carry

        lax.fori_loop(0, end, step, 0)

    def go_on(self, first, end):
        def distance(k):
            return k // 2 + 1 + (NEAR - 1) * (k % 2)

        def step(k, carry):
            self.along_z(distance(k), k != NZ - 2)
            return carry

        lax.fori_loop(first, end, step, 0)

    def crossings(self, act):
        for dx in range(NX):
            for q in range(2 if dx == 0 else NZ // PAIR):
                act(dx, q)

    def finish(self, own):
        own.wait()
        for q in range(2):
            self.cross(0, q).start()
        self.pairs(self.along_x)
        self.pairs(self.last_halves)
        self.crossings(lambda dx, q: self.cross(dx, q, True).wait_recv())

    def drain(self):
        z = self.p.z
        self.crossings(lambda dx, q: self.cross(dx, q).wait_send())

        def sent(k, carry):
            for way in range(2):
                self.x_forward(k, way).wait_send()
                self.x_copy(k, way).wait_send()
            on = jnp.logical_and(k != NEAR - 1, jnp.logical_and(self.has_up, k <= z))
            back = jnp.logical_and(k != NEAR - 1, jnp.logical_and(self.has_down, k <= NZ - 1 - z))
            for b in range(2):
                pl.when(on)(lambda b=b: self.z_up(k, b).wait_send())
                pl.when(back)(lambda b=b: self.z_down(k, b).wait_send())
            return carry

        lax.fori_loop(0, NZ, sent, 0)
        for b in range(2):
            pl.when(self.far_up)(lambda b=b: self.z_up(0, b, True, NEAR).wait_send())
            pl.when(self.far_down)(lambda b=b: self.z_down(0, b, True, NEAR).wait_send())


def find_links(coords, live, plan_ref):
    slots, wide = coords.shape[1], plan_ref.shape[1]
    rows = jnp.broadcast_to(coords[0:1, :], (slots, slots))
    down = lax.broadcasted_iota(jnp.int32, (slots, slots), 0)
    across = lax.broadcasted_iota(jnp.int32, (slots, slots), 1)
    row_of = jnp.sum(jnp.where(down == across, rows, 0), axis=1, keepdims=True)
    earlier = jnp.logical_and(row_of == rows, down < across)
    before = jnp.max(jnp.where(earlier, down, -1), axis=0, keepdims=True)
    plan_ref[...] = jnp.full(plan_ref.shape, slots, jnp.int32)
    plan_ref[0:1, 0:slots] = jnp.where(before < 0, slots, before)
    cols = coords[1:2, :]
    core = (cols // 2) % NC
    plan_ref[0:1, slots : 2 * slots] = (core * NX * NZ + cols // (2 * NC)) * 2 + cols % 2
    place = lax.broadcasted_iota(jnp.int32, (slots, wide), 1)
    slot = lax.broadcasted_iota(jnp.int32, (slots, wide), 0)
    named = jnp.logical_and(row_of == place, slot < live)
    last = jnp.max(jnp.where(named, slot, -1), axis=0, keepdims=True)
    plan_ref[1:2, :] = jnp.where(last < 0, slots, last)


def multiply(plan, adj_v, feat_v, sums):
    def turn(g, carry):
        first = g * UNROLL
        products = [
            jnp.dot(adj_v[first + i], feat_v[plan[0, adj_v.shape[0] + first + i]], preferred_element_type=F32)
            for i in range(UNROLL)
        ]
        for i in range(UNROLL):
            sums[first + i] = products[i] + sums[plan[0, first + i]]
        return carry

    lax.fori_loop(0, adj_v.shape[0] // UNROLL, turn, 0)


def reduce_rows(p, plan, sums, ysend, yrecv, zsend, zrecv, own_ref, ys_s, ys_r, zs_s, zs_r):
    half = sums.shape[1]

    def part(dy, k, b):
        block_row = (((p.y + dy) % NY) * NH + (p.h + k) % NH) * 2 + b
        return sums[plan[1, block_row]]

    def y_copy(k, dy):
        i = dy - 1
        return remote(ysend.at[k, i], yrecv.at[k, i], ys_s.at[k, i], ys_r.at[k, i], p.at_y(p.y + dy))

    def y_start(k):
        for dy in (2, 1, 3):
            for b in range(2):
                ysend[k, dy - 1, pl.ds(b * half, half)] = part(dy, k, b).astype(BF16)
            y_copy(k, dy).start()

    def y_end(k):
        for dy in range(1, NY):
            y_copy(k, dy).wait_recv()

    def y_sum(k, b):
        total = part(0, k, b)
        for i in range(NY - 1):
            total = total + yrecv[k, i, pl.ds(b * half, half)].astype(F32)
        return total

    def z_copy(i):
        device = p.at_h(p.h + (1 if i % 2 == 0 else NH - 1))
        return remote(zsend.at[i], zrecv.at[i], zs_s.at[i], zs_r.at[i], device)

    def z_start(i, value):
        zsend[i] = value.astype(BF16)
        z_copy(i).start()

    y_start(2)
    y_start(1)
    y_end(2)
    z_start(0, y_sum(2, 0))
    z_start(1, y_sum(2, 1))
    y_start(3)
    y_start(0)
    y_end(1)
    z_start(2, y_sum(1, 1))
    y_end(3)
    z_start(3, y_sum(3, 0))
    own_ref[0] = y_sum(1, 0)
    own_ref[1] = y_sum(3, 1)
    z_copy(0).wait_recv()
    z_start(4, own_ref[0] + zrecv[0].astype(F32))
    z_copy(1).wait_recv()
    z_start(5, own_ref[1] + zrecv[1].astype(F32))
    y_end(0)
    own_ref[0] = y_sum(0, 0)
    own_ref[1] = y_sum(0, 1)

    def drain():
        for k in range(NH):
            for dy in range(1, NY):
                y_copy(k, dy).wait_send()
        for i in range(6):
            z_copy(i).wait_send()

    def total(b):
        first, second = ((3, 4), (2, 5))[b]
        z_copy(first).wait_recv()
        z_copy(second).wait_recv()
        return own_ref[b] + zrecv[first].astype(F32) + zrecv[second].astype(F32)

    return total, drain


def silu_slope(preact, sigmoid_value):
    return sigmoid_value * (1.0 + preact * (1.0 - sigmoid_value))


def apply_layer(rounded, weight, cotangent, act_ref, grad_v):
    preact = jnp.dot(rounded, weight, preferred_element_type=F32)
    sigmoid_value = 1.0 / (1.0 + jnp.exp(-preact))
    act_ref[...] = (preact * sigmoid_value).astype(BF16)
    slope_grad = (cotangent.astype(F32) * silu_slope(preact, sigmoid_value)).astype(BF16)
    local_grad = lax.dot_general(rounded, slope_grad, (((0,), (0,)), ((), ())), preferred_element_type=F32)
    members, chunk, lanes = grad_v.shape
    per = members * lanes // local_grad.shape[1]
    for i in range(members // per):
        grad_v[i * per : (i + 1) * per] = local_grad[:, i * lanes : (i + 1) * lanes].reshape(per, chunk, lanes)


def sum_gradient(p, grad_v, r1, c1, r2, c2, r3, c3, r4, g_s, g_r, meanwhile):
    far = p.tall // NEAR

    def all_of(count, k):
        return remote(r1.at[:count], r1.at[:count], g_s.at[k], g_r.at[k], p.member(p.me))

    def scatter(j, carry):
        m = (p.me + j) % p.members
        remote(grad_v.at[m], r1.at[j - 1], g_s.at[0], g_r.at[0], p.member(m)).start()
        return carry

    lax.fori_loop(1, p.members, scatter, 0)
    all_of(p.members - 1, 0).wait_recv()
    c1[...] = grad_v[p.me] + jnp.sum(r1[...], axis=0)
    for j in range(1, NEAR):
        there = p.at_level(p.team * NEAR + (p.near + j) % NEAR)
        remote(c1, r2.at[p.near], g_s.at[1], g_r.at[1], there).start()
    r2[p.near] = c1[...]
    all_of(NEAR - 1, 1).wait_recv()
    c2[...] = jnp.sum(r2[...], axis=0)
    for j in sorted(range(1, far), key=lambda j: -min(j, far - j)):
        remote(c2, r3.at[p.team], g_s.at[2], g_r.at[2], p.up(j * NEAR)).start()
    r3[p.team] = c2[...]
    meanwhile()
    all_of(p.members - 1, 0).wait_send()
    all_of(NEAR - 1, 1).wait_send()
    all_of(far - 1, 2).wait_recv()
    c3[...] = jnp.sum(r3[...], axis=0)

    def hand_out(j, carry):
        remote(c3, r4.at[p.me], g_s.at[3], g_r.at[3], p.member((p.me + j) % p.members)).start()
        return carry

    lax.fori_loop(1, p.members, hand_out, 0)
    r4[p.me] = c3[...]
    all_of(far - 1, 2).wait_send()
    all_of(p.members - 1, 3).wait_recv()
    all_of(p.members - 1, 3).wait_send()


def write_gradient(r4, grad_ref):
    members, chunk, lanes = r4.shape
    per = grad_ref.shape[0] // chunk
    for i in range(members // per):
        grad_ref[:, i * lanes : (i + 1) * lanes] = r4[i * per : (i + 1) * per].reshape(per * chunk, lanes)


def gather_scratch(rows, width):
    dma = pltpu.SemaphoreType.DMA
    return (
        [pltpu.VMEM((2 * NX * NZ * NC, rows // 2, width), BF16)]
        + [dma((NZ, 2))] * 4
        + [dma((2, NZ))] * 4
        + [dma((NX, NZ // PAIR))] * 2
    )


def reduce_scratch(rows, width):
    dma = pltpu.SemaphoreType.DMA
    half = rows // 2
    return (
        [pltpu.VMEM((NH, NY - 1, rows, width), BF16)] * 2
        + [pltpu.VMEM((6, half, width), BF16)] * 2
        + [pltpu.VMEM((2, half, width), F32)]
        + [dma((NH, NY - 1))] * 2
        + [dma((6,))] * 2
    )


def gradient_scratch(size):
    dma = pltpu.SemaphoreType.DMA
    members, lanes = NX * NY * NC, 128
    chunk = (size // members // lanes, lanes)
    return [
        pltpu.VMEM((count,) + chunk if count else chunk, F32)
        for count in (members, members - 1, 0, NEAR, 0, NZ * NH // NEAR, 0, members)
    ] + [dma((4,))] * 2


def whole_kernel(f_ref, adj_ref, coords_ref, counts_ref, w_ref, cot_ref, act_ref, grad_ref, *scratch):
    adj_v, coords_v, counts_s, plan_v, plan_s, w_v, cot_v, sums, in_sem, told, feat_v, *rest = scratch
    gather_sems, rest = rest[:10], rest[10:]
    reduce_refs, gradient_refs = rest[:9], rest[9:]
    p = Place()
    slots = adj_v.shape[0]
    pairs = (
        (coords_ref, coords_v), (counts_ref, counts_s),
        (f_ref, feat_v.at[pl.ds(2 * p.shelf(p.x, p.z), 2)]),
        (adj_ref, adj_v), (w_ref, w_v), (cot_ref, cot_v),
    )
    fetches = [pltpu.make_async_copy(a, b, in_sem.at[i]) for i, (a, b) in enumerate(pairs)]
    meet(p)
    gather = Gather(p, f_ref, feat_v, *gather_sems)
    gather.begin()
    tell(p, told)
    for fetch in fetches:
        fetch.start()
    gather.go_on(0, 2)
    sums[slots] = jnp.zeros(sums.shape[1:], F32)
    for fetch in fetches[:2]:
        fetch.wait()
    find_links(coords_v[...], counts_s[p.c, p.r], plan_v)
    links = pltpu.make_async_copy(plan_v, plan_s, in_sem.at[0])
    links.start()
    gather.go_on(2, NZ)
    links.wait()
    hear(p, told)
    for fetch in fetches[3:]:
        fetch.wait()
    gather.finish(fetches[2])
    multiply(plan_s, adj_v, feat_v, sums)
    total, reduce_drain = reduce_rows(p, plan_s, sums, *reduce_refs)
    rounded = jnp.concatenate([total(0).astype(BF16), total(1).astype(BF16)], axis=0)
    apply_layer(rounded, w_v[...], cot_v[...], act_ref, gradient_refs[0])

    def drain():
        gather.drain()
        reduce_drain()

    sum_gradient(p, *gradient_refs, drain)
    write_gradient(gradient_refs[7], grad_ref)


def body(features, adj_blocks, block_coords, counts, weight, cotangent):
    tile_blocks, tile_coords = adj_blocks[0, 0], block_coords[0, 0]
    slots, block, _ = tile_blocks.shape
    rows, width = features.shape
    dma = pltpu.SemaphoreType.DMA
    vmem, hbm = pl.BlockSpec(memory_space=pltpu.VMEM), pl.BlockSpec(memory_space=pl.ANY)
    return pl.pallas_call(
        whole_kernel,
        out_shape=(
            jax.ShapeDtypeStruct(cotangent.shape, BF16),
            jax.ShapeDtypeStruct(weight.shape, F32),
        ),
        in_specs=[hbm] * 6,
        out_specs=(vmem, vmem),
        scratch_shapes=[
            pltpu.VMEM(tile_blocks.shape, BF16),
            pltpu.VMEM(tile_coords.shape, jnp.int32),
            pltpu.SMEM(counts.shape[::-1], jnp.int32),
            pltpu.VMEM((2, 128), jnp.int32),
            pltpu.SMEM((2, 128), jnp.int32),
            pltpu.VMEM(weight.shape, BF16),
            pltpu.VMEM(cotangent.shape, BF16),
            pltpu.VMEM((slots + 1, block, width), F32),
            dma((6,)),
            pltpu.SemaphoreType.REGULAR,
        ]
        + gather_scratch(rows, width)
        + reduce_scratch(rows, width)
        + gradient_scratch(weight.size),
        compiler_params=pltpu.CompilerParams(
            collective_id=0, has_side_effects=True, vmem_limit_bytes=60 << 20
        ),
        name="graph_convolution",
    )(features.reshape(2, rows // 2, width), tile_blocks, tile_coords, counts.T, weight, cotangent)


def solution(mesh):
    return jax.shard_map(
        body,
        mesh=mesh,
        in_specs=(
            P(("col", "row"), None),
            P("row", "col", None, None, None),
            P("row", "col", None, None),
            P(),
            P(),
            P(("row", "col"), None),
        ),
        out_specs=(P(("row", "col"), None), P()),
        check_vma=False,
    )
```
